256 devices in a mesh: gx: 16 (over y_lo, z), gy: 16 (over x, y_hi, core).
Axes of the slice: x: 4, y: 4 (y_hi: 2, y_lo: 2; y = y_hi * 2 + y_lo), z: 8, core: 2. Of those that a mesh axis runs over, the one named last changes fastest.
Arguments:
- object_field: float32 [2, 4096, 4096], P(None, 'gy', 'gx'), may hold values from -5 to 5
- probe: float32 [3, 2, 256, 256], replicated, may hold values from -5 to 5
- amplitudes: float32 [16, 16, 4, 256, 256], P('gy', 'gx'), may hold values from 0 to 3
- positions: int32 [16, 16, 4, 2], P('gy', 'gx'), may hold values from 0 to 3840, as said below
- counts: int32 [16, 16], replicated, may hold values from 1 to 4, as said below
Outputs:
- new_object: float32 [2, 4096, 4096], P(None, 'gy', 'gx')
- new_probe: float32 [3, 2, 256, 256], replicated
The draws below stay inside these ranges and needn't reach their ends.
Inputs may be any that keep to these rules, and one draw needn't show every extreme that they name: `positions`: every slot's patch lies inside the object, and its corner lies in the tile (rows a * 256 on, columns b * 256 on) of the slot's own (a, b); dead slots obey this too. Live slots are the first counts[a, b] of a tile; some tile has exactly 4.
All inputs are finite; a program needn't handle non-finite values.
Results may differ from the reference program's by a relative error of at most 0.0001.
Values sent between devices are 32-bit elements; how exact they have to be, the bound alone decides.
No kernel may reach another device: no remote copies, remote signals or barrier semaphores. Data moves between devices by JAX's collectives and lax.ppermute only.
A program may use at most 192 MiB of HBM per device.

```python
import jax
import jax.numpy as jnp
from jax import lax

PATCH = 256
MODES = 3
TILE_R = 256
TILE_C = 256
CAP = 4
OBJ_ROWS = 4096
OBJ_COLS = 4096
N_GX = 16
N_GY = 16


def draw_positions(key, part):
    key = jax.random.fold_in(key, 11)
    row_key, col_key = jax.random.split(key)
    tile_row = jnp.arange(N_GY, dtype=jnp.int32)[:, None, None]
    tile_col = jnp.arange(N_GX, dtype=jnp.int32)[None, :, None]
    slot_ids = jnp.arange(CAP, dtype=jnp.int32)[None, None, :]
    grid_shape = (N_GY, N_GX, CAP)
    row_limit = jnp.broadcast_to(jnp.where(tile_row == N_GY - 1, TILE_R - PATCH + 1, TILE_R), grid_shape)
    col_limit = jnp.broadcast_to(jnp.where(tile_col == N_GX - 1, TILE_C - PATCH + 1, TILE_C), grid_shape)
    row_offset = jax.random.randint(row_key, grid_shape, 0, row_limit)
    col_offset = jax.random.randint(col_key, grid_shape, 0, col_limit)
    rows_global = tile_row * TILE_R + row_offset
    cols_global = tile_col * TILE_C + col_offset
    first_slot = (tile_row == 0) & (tile_col == 0) & (slot_ids == 0)
    last_slot = (tile_row == N_GY - 1) & (tile_col == N_GX - 1) & (slot_ids == 0)
    rows_global = jnp.where(first_slot, 0, jnp.where(last_slot, N_GY * TILE_R - PATCH, rows_global))
    cols_global = jnp.where(first_slot, 0, jnp.where(last_slot, N_GX * TILE_C - PATCH, cols_global))
    return jnp.stack([rows_global, cols_global], -1).astype(jnp.int32)


def draw_counts(key, part):
    key = jax.random.fold_in(key, 23)
    first_key, second_key, spot_key = jax.random.split(key, 3)
    first_draw = jax.random.randint(first_key, (N_GY, N_GX), 0, CAP // 2 + 1)
    second_draw = jax.random.randint(second_key, (N_GY, N_GX), 0, CAP // 2 + 1)
    base_count = jnp.maximum(CAP - jnp.minimum(first_draw, second_draw), 1)
    spot_index = jax.random.randint(spot_key, (), 0, N_GY * N_GX)
    flat_count = base_count.reshape(-1).at[spot_index].set(CAP)
    return flat_count.reshape(N_GY, N_GX).astype(jnp.int32)


def level_of(stream_key, extent, cuts, smallest, largest):
    level, own = 1.0, jax.random.fold_in(stream_key, 6)
    for dim, parts in cuts:
        draws = jnp.exp(jax.random.uniform(jax.random.fold_in(own, dim), (parts,), jnp.float32, smallest / len(cuts), largest / len(cuts)))
        level = level * jnp.repeat(draws, extent[dim] // parts).reshape([-1 if axis == dim else 1 for axis in range(len(extent))])
    return level


def bell_draw(key, dims, spread, bound, cuts=(), kind=jnp.bfloat16):
    entries = spread * jax.random.normal(key, dims, jnp.float32)
    if cuts:
        entries = entries * level_of(key, dims, cuts, -0.22, 0.18)
    return jnp.clip(entries, -bound, bound).astype(kind)


def setup_inputs(seed: int = 0) -> dict:
    keys = jax.random.split(jax.random.key(seed), 6)
    object_field = bell_draw(keys[0], (2, OBJ_ROWS, OBJ_COLS), 0.7, 5.0, ((1, 16), (2, 16)), jnp.float32)
    probe = bell_draw(keys[1], (MODES, 2, PATCH, PATCH), 0.6, 5.0, (), jnp.float32)
    amplitudes = jnp.clip(3.0 * jax.random.uniform(keys[2], (N_GY, N_GX, CAP, PATCH, PATCH), jnp.float32) ** level_of(keys[2], (N_GY, N_GX, CAP, PATCH, PATCH), ((0, 16), (1, 16)), -0.2, 0.2), 0.0, 3.0)
    positions = draw_positions(jax.random.fold_in(keys[5], 71), 0)
    counts = draw_counts(jax.random.fold_in(keys[5], 71), 0)
    return {"object_field": object_field, "probe": probe, "amplitudes": amplitudes, "positions": positions, "counts": counts}


def reference(object_field, probe, amplitudes, positions, counts):
    object_wave = object_field[0] + 1j * object_field[1]
    probe_wave = probe[:, 0] + 1j * probe[:, 1]
    coverage = lax.optimization_barrier(jnp.sum(probe * probe, axis=(0, 1)))
    slot_index = jnp.arange(CAP, dtype=jnp.int32)
    live_mask = (slot_index[None, None, :] < counts[:, :, None]).astype(object_field.dtype).reshape(-1)
    corners = positions.reshape(-1, 2)
    measured = amplitudes.reshape(-1, PATCH, PATCH)

    def visit_item(carry, item):
        gradient, weight_sum, probe_grad, density = carry
        corner, amplitude, live = item
        row_at = corner[0]
        col_at = corner[1]
        patch_block = lax.dynamic_slice(object_wave, (row_at, col_at), (PATCH, PATCH))
        exit_wave = probe_wave * patch_block[None]
        far_wave = jnp.fft.fft2(exit_wave, norm='ortho')
        intensity = lax.optimization_barrier(jnp.sum(jnp.real(far_wave) ** 2 + jnp.imag(far_wave) ** 2, axis=0))
        factor = amplitude / jnp.maximum(jnp.sqrt(intensity), 0.5)
        back_wave = jnp.fft.ifft2(far_wave * factor[None], norm='ortho')
        difference = (exit_wave - back_wave) * live
        object_part = lax.optimization_barrier(jnp.sum(jnp.conj(probe_wave) * difference, axis=0))
        current = lax.dynamic_slice(gradient, (row_at, col_at), (PATCH, PATCH))
        gradient = lax.dynamic_update_slice(gradient, current + object_part, (row_at, col_at))
        current_weight = lax.dynamic_slice(weight_sum, (row_at, col_at), (PATCH, PATCH))
        weight_sum = lax.dynamic_update_slice(weight_sum, current_weight + coverage * live, (row_at, col_at))
        probe_grad = probe_grad + jnp.conj(patch_block)[None] * difference
        density = density + (jnp.real(patch_block) ** 2 + jnp.imag(patch_block) ** 2) * live
        return ((gradient, weight_sum, probe_grad, density), None)
    start = (jnp.zeros_like(object_wave), jnp.zeros_like(object_field[0]), jnp.zeros_like(probe_wave), jnp.zeros((PATCH, PATCH), object_field.dtype))
    final, unused = lax.scan(visit_item, start, (corners, measured, live_mask))
    gradient, weight_sum, probe_grad, density = final
    updated_object = object_wave - gradient / (weight_sum + 1.0)
    updated_probe = probe_wave - probe_grad / (density + 1.0)[None]
    new_object = jnp.stack([jnp.real(updated_object), jnp.imag(updated_object)], 0)
    new_probe = jnp.stack([jnp.real(updated_probe), jnp.imag(updated_probe)], 1)
    return (new_object, new_probe)
```

```python
import math

import jax
import jax.numpy as jnp
import numpy as np
from jax import lax
from jax.experimental import pallas as pl
from jax.experimental.pallas import tpu as pltpu
from jax.sharding import PartitionSpec as P

SIDE = 256
HALF = 128
MODES = 3
SLOTS = 4
PLANES = 2 * MODES + 1
AXES = ("gx", "gy")
VMEM = pltpu.VMEM
SMEM = pltpu.SMEM
F32 = jnp.float32
BF16 = jnp.bfloat16


def flat_index(x, y, z, core):
    return ((y % 2) * 8 + z) * 16 + x * 4 + (y // 2) * 2 + core


def routes(move):
    pairs = []
    for x in range(4):
        for y in range(4):
            for z in range(8):
                for core in range(2):
                    tx, ty, tz, tc = move(x, y, z, core)
                    pairs.append((flat_index(x, y, z, core), flat_index(tx % 4, ty % 4, tz % 8, tc % 2)))
    return pairs


def first_ring(step):
    return routes(lambda x, y, z, c: (x + step, y, z, c) if c == 0 else (x, y + step, z, c))


def second_ring(step):
    return routes(lambda x, y, z, c: (x, y + step, z, c) if c == 0 else (x + step, y, z, c))


def depth_ring(step):
    return routes(lambda x, y, z, c: (x, y, z + step, c))


def depth_pair():
    return routes(lambda x, y, z, c: (x, y, z ^ 1, c))


def core_pair():
    return routes(lambda x, y, z, c: (x, y, z, 1 - c))


def send(value, pairs):
    return lax.ppermute(value, AXES, pairs)


def shifted(value, axis, steps):
    count = lax.axis_size(axis)
    leading, last = (max(0, -steps), min(count, count - steps))
    return lax.ppermute(value, axis, [(source, source + steps) for source in range(leading, last)])


def split_table(matrix):
    high = matrix.astype(np.float32).astype(jnp.bfloat16)
    low = (matrix - high.astype(np.float64)).astype(jnp.bfloat16)
    return high, low


def transform_tables():
    n = np.arange(HALF)[:, None].astype(np.int64)
    k = np.arange(HALF)[None, :].astype(np.int64)
    tables = []
    for odd in (0, 1):
        angle = (n * (2 * k + odd) % SIDE) * (-2.0 * math.pi / SIDE)
        cos, sin = np.cos(angle) / 16.0, np.sin(angle) / 16.0
        right = np.block([[cos, sin], [-sin, cos]])
        for matrix in (right, right.T):
            tables.extend(split_table(matrix))
    return np.stack(tables)


def order_table():
    table = np.zeros((SIDE, SIDE), np.float32)
    order = np.concatenate([np.arange(0, SIDE, 2), np.arange(1, SIDE, 2)])
    table[order, np.arange(SIDE)] = 1.0
    return table.astype(jnp.bfloat16)


def split(value):
    high = value.astype(BF16)
    low = (value - high.astype(F32)).astype(BF16)
    return high, low


def dot(left, right):
    return jnp.dot(left, right, preferred_element_type=F32)


def apply_right(value, table, which):
    high, low = split(value)
    return dot(low, table[which]) + dot(high, table[which + 1]) + dot(high, table[which])


def apply_left(table, which, value):
    high, low = split(value)
    return dot(table[which], low) + dot(table[which + 1], high) + dot(table[which], high)


def lanes(*parts):
    return jnp.concatenate(parts, axis=1)


def rows(*parts):
    return jnp.concatenate(parts, axis=0)


def prepare_kernel(place, counts, own, left, above, corner, probe, amplitude, order, amp_out, weight_out, doubled, measured, sems):
    loads = [
        pltpu.make_async_copy(
            amplitude.at[:, :, pl.ds(block * HALF, HALF)], measured.at[:, block], sems.at[block]
        )
        for block in range(2)
    ]
    for load in loads:
        load.start()
    for load in loads:
        load.wait()
    for item in range(SLOTS):
        sorted_rows = lanes(
            *[
                rows(*[measured[item, block, pl.ds(odd, HALF, stride=2), :] for odd in range(2)])
                for block in range(2)
            ]
        )
        high, rest = split(sorted_rows)
        rest32 = sorted_rows - high.astype(F32)
        middle, low = split(rest32)
        amp_out[item] = dot(high, order[...]) + (dot(middle, order[...]) + dot(low, order[...]))
    coverage = probe[0, 0] * probe[0, 0]
    for mode in range(MODES):
        for part in range(2):
            if mode or part:
                coverage = coverage + probe[mode, part] * probe[mode, part]
    for block in range(2):
        for start in (0, SIDE):
            doubled[block, pl.ds(start, SIDE), :] = coverage[:, block * HALF : (block + 1) * HALF]
    row_id = place[0]
    col_id = place[1]
    row_iota = lax.broadcasted_iota(jnp.int32, (SIDE, SIDE), 0)
    lane_iota = lax.broadcasted_iota(jnp.int32, (SIDE, SIDE), 1)
    weight_out[...] = jnp.ones((SIDE, SIDE), F32)
    for up, back, points in ((0, 0, own), (0, 1, left), (1, 0, above), (1, 1, corner)):
        tile_row = row_id - up
        tile_col = col_id - back
        inside = jnp.logical_and(tile_row >= 0, tile_col >= 0)
        count = jnp.where(inside, counts[jnp.maximum(tile_row, 0), jnp.maximum(tile_col, 0)], 0)

        def visit(item, carry, points=points, tile_row=tile_row, tile_col=tile_col, up=up, back=back):
            row_at = points[item, 0] - tile_row * SIDE
            col_at = points[item, 1] - tile_col * SIDE
            window = pl.ds(SIDE - row_at, SIDE)
            moved = pltpu.roll(lanes(doubled[0, window, :], doubled[1, window, :]), col_at, 1)
            row_ok = row_iota < row_at if up else row_iota >= row_at
            col_ok = lane_iota < col_at if back else lane_iota >= col_at
            weight_out[...] += jnp.where(jnp.logical_and(row_ok, col_ok), moved, 0.0)
            return carry

        lax.fori_loop(0, count, visit, 0)


def prepare(place, counts, own, left, above, corner, probe, amplitude, order):
    return pl.pallas_call(
        prepare_kernel,
        out_shape=(
            jax.ShapeDtypeStruct((SLOTS, SIDE, SIDE), F32),
            jax.ShapeDtypeStruct((SIDE, SIDE), F32),
        ),
        in_specs=[pl.BlockSpec(memory_space=SMEM)] * 6
        + [pl.BlockSpec(memory_space=VMEM), pl.BlockSpec(memory_space=pl.ANY), pl.BlockSpec(memory_space=VMEM)],
        out_specs=(pl.BlockSpec(memory_space=VMEM),) * 2,
        scratch_shapes=[
            VMEM((2, 2 * SIDE, HALF), F32),
            VMEM((SLOTS, 2, SIDE, HALF), F32),
            pltpu.SemaphoreType.DMA((2,)),
        ],
        compiler_params=pltpu.CompilerParams(vmem_limit_bytes=32 * 1024 * 1024),
        cost_estimate=pl.CostEstimate(flops=2_000_000_000, bytes_accessed=4_000_000, transcendentals=0),
        name="prepare",
    )(place, counts, own, left, above, corner, probe, amplitude, order)


def pattern_kernel(
    place, counts, points, own, right, lower, corner, probe, amplitude, table,
    core_out, right_out, lower_out, corner_out, send_out, keep_out,
    field, target, total, spectrum, sems,
):
    row_id = place[0]
    col_id = place[1]
    core = place[2]
    loads = []
    for piece, up, back in ((own, 0, 0), (right, 0, 1), (lower, 1, 0), (corner, 1, 1)):
        for block in range(2):
            loads.append(
                pltpu.make_async_copy(
                    piece.at[:, :, pl.ds(block * HALF, HALF)],
                    field.at[:, 2 * back + block, pl.ds(up * SIDE, SIDE), :],
                    sems.at[len(loads)],
                )
            )
    for load in loads:
        load.start()
    target[...] = jnp.zeros_like(target)
    total[...] = jnp.zeros_like(total)
    for load in loads:
        load.wait()
    lane_iota = lax.broadcasted_iota(jnp.int32, (SIDE, SIDE), 1)

    def visit(item, carry):
        row_at = points[item, 0] - row_id * SIDE
        col_at = points[item, 1] - col_id * SIDE
        in_left = lane_iota >= col_at
        rest = jnp.where(col_at == 0, 0, SIDE - col_at)

        def cut(part):
            window = pl.ds(row_at, SIDE)
            first = lanes(field[part, 0, window, :], field[part, 1, window, :])
            second = lanes(field[part, 2, window, :], field[part, 3, window, :])
            return pltpu.roll(jnp.where(in_left, first, second), rest, 1)

        object_real = cut(0)
        object_imag = cut(1)
        density = object_real * object_real + object_imag * object_imag
        total[:, PLANES - 1] += density.reshape(32, 8, SIDE)

        even_sum = jnp.zeros((HALF, SIDE), F32)
        odd_sum = jnp.zeros((HALF, SIDE), F32)
        for mode in range(MODES):
            probe_real = probe[mode, 0]
            probe_imag = probe[mode, 1]
            real = probe_real * object_real - probe_imag * object_imag
            imag = probe_real * object_imag + probe_imag * object_real
            even = apply_right(
                lanes(real[:, :HALF] + real[:, HALF:], imag[:, :HALF] + imag[:, HALF:]), table, 0
            )
            odd = apply_right(
                lanes(real[:, :HALF] - real[:, HALF:], imag[:, :HALF] - imag[:, HALF:]), table, 4
            )
            real = lanes(even[:, :HALF], odd[:, :HALF])
            imag = lanes(even[:, HALF:], odd[:, HALF:])
            even = apply_left(table, 2, rows(real[:HALF] + real[HALF:], imag[:HALF] + imag[HALF:]))
            odd = apply_left(table, 6, rows(real[:HALF] - real[HALF:], imag[:HALF] - imag[HALF:]))
            spectrum[mode, 0] = even
            spectrum[mode, 1] = odd
            even_sum += even[:HALF] * even[:HALF] + even[HALF:] * even[HALF:]
            odd_sum += odd[:HALF] * odd[:HALF] + odd[HALF:] * odd[HALF:]
        even_factor = amplitude[item, :HALF] / jnp.maximum(jnp.sqrt(even_sum), 0.5)
        odd_factor = amplitude[item, HALF:] / jnp.maximum(jnp.sqrt(odd_sum), 0.5)
        even_factor = rows(even_factor, even_factor)
        odd_factor = rows(odd_factor, odd_factor)
        grad_real = jnp.zeros((SIDE, SIDE), F32)
        grad_imag = jnp.zeros((SIDE, SIDE), F32)
        for mode in range(MODES):
            even = apply_left(table, 0, spectrum[mode, 0] * even_factor)
            odd = apply_left(table, 4, spectrum[mode, 1] * odd_factor)
            high = even + odd
            low = even - odd
            real = rows(high[:HALF], low[:HALF])
            imag = rows(high[HALF:], low[HALF:])
            even = apply_right(lanes(real[:, :HALF], imag[:, :HALF]), table, 2)
            odd = apply_right(lanes(real[:, HALF:], imag[:, HALF:]), table, 6)
            high = even + odd
            low = even - odd
            real = lanes(high[:, :HALF], low[:, :HALF])
            imag = lanes(high[:, HALF:], low[:, HALF:])
            probe_real = probe[mode, 0]
            probe_imag = probe[mode, 1]
            grad_real += probe_real * real + probe_imag * imag
            grad_imag += probe_real * imag - probe_imag * real
            total[:, 2 * mode] += (object_real * real + object_imag * imag).reshape(32, 8, SIDE)
            total[:, 2 * mode + 1] += (object_real * imag - object_imag * real).reshape(32, 8, SIDE)
        for part, grad in ((0, grad_real), (1, grad_imag)):
            moved = pltpu.roll(grad, col_at, 1)
            first = jnp.where(in_left, moved, 0.0)
            second = jnp.where(in_left, 0.0, moved)
            window = pl.ds(row_at, SIDE)
            for block, piece in enumerate((first[:, :HALF], first[:, HALF:], second[:, :HALF], second[:, HALF:])):
                target[part, block, window, :] += piece
        return carry

    lax.fori_loop(0, counts[row_id, col_id], visit, 0)
    stores = [
        pltpu.make_async_copy(total.at[pl.ds((1 - core) * 16, 16)], send_out, sems.at[0]),
        pltpu.make_async_copy(total.at[pl.ds(core * 16, 16)], keep_out, sems.at[1]),
    ]
    for piece, up, back in ((core_out, 0, 0), (right_out, 0, 1), (lower_out, 1, 0), (corner_out, 1, 1)):
        for block in range(2):
            stores.append(
                pltpu.make_async_copy(
                    target.at[:, 2 * back + block, pl.ds(up * SIDE, SIDE), :],
                    piece.at[:, :, pl.ds(block * HALF, HALF)],
                    sems.at[len(stores)],
                )
            )
    for store in stores:
        store.start()
    for store in stores:
        store.wait()


def visit_patterns(place, counts, points, own, right, lower, corner, probe, amplitude, table):
    tile = jax.ShapeDtypeStruct((2, SIDE, SIDE), F32)
    part = jax.ShapeDtypeStruct((16, PLANES, 8, SIDE), F32)
    return pl.pallas_call(
        pattern_kernel,
        out_shape=(tile, tile, tile, tile, part, part),
        in_specs=[pl.BlockSpec(memory_space=SMEM)] * 3
        + [pl.BlockSpec(memory_space=pl.ANY)] * 4
        + [pl.BlockSpec(memory_space=VMEM)] * 3,
        out_specs=(pl.BlockSpec(memory_space=pl.ANY),) * 6,
        scratch_shapes=[
            VMEM((2, 4, 2 * SIDE, HALF), F32),
            VMEM((2, 4, 2 * SIDE, HALF), F32),
            VMEM((32, PLANES, 8, SIDE), F32),
            VMEM((MODES, 2, SIDE, SIDE), F32),
            pltpu.SemaphoreType.DMA((10,)),
        ],
        compiler_params=pltpu.CompilerParams(vmem_limit_bytes=48 * 1024 * 1024),
        cost_estimate=pl.CostEstimate(flops=10_000_000_000, bytes_accessed=10_000_000, transcendentals=0),
        name="patterns",
    )(place, counts, points, own, right, lower, corner, probe, amplitude, table)


def scatter_kernel(slot, place, *refs):
    pieces, outs = refs[:-4], refs[-4:]
    length = outs[0].shape[0]
    mine = place[slot]
    for step in range(4):
        start = lax.rem(mine + step, 4) * length
        block = pieces[0][pl.ds(start, length)]
        for piece in pieces[1:]:
            block = block + piece[pl.ds(start, length)]
        outs[step][...] = block


def scatter_sum(slot, place, pieces):
    shape = (pieces[0].shape[0] // 4,) + pieces[0].shape[1:]

    def body(*refs):
        scatter_kernel(slot, *refs)

    return pl.pallas_call(
        body,
        out_shape=(jax.ShapeDtypeStruct(shape, F32),) * 4,
        in_specs=[pl.BlockSpec(memory_space=SMEM)] + [pl.BlockSpec(memory_space=VMEM)] * len(pieces),
        out_specs=(pl.BlockSpec(memory_space=VMEM),) * 4,
        compiler_params=pltpu.CompilerParams(vmem_limit_bytes=32 * 1024 * 1024),
        name="scatter_sum",
    )(place, *pieces)


def plain_sum(pieces):
    def body(*refs):
        block = refs[0][...]
        for piece in refs[1:-1]:
            block = block + piece[...]
        refs[-1][...] = block

    return pl.pallas_call(
        body,
        out_shape=jax.ShapeDtypeStruct(pieces[0].shape, F32),
        in_specs=[pl.BlockSpec(memory_space=VMEM)] * len(pieces),
        out_specs=pl.BlockSpec(memory_space=VMEM),
        name="plain_sum",
    )(*pieces)


def update_probe(place, pieces, probe):
    def body(place, *refs):
        probe_ref, out = refs[-2], refs[-1]
        block = refs[0][0]
        for piece in refs[1:-2]:
            block = block + piece[0]
        group = place[2] * 16 + place[3] * 4 + place[4]
        scale = 1.0 / (block[PLANES - 1] + 1.0)
        for plane in range(PLANES - 1):
            out[0, plane] = (probe_ref[plane, group] + block[plane]) * scale

    return pl.pallas_call(
        body,
        out_shape=jax.ShapeDtypeStruct((1, PLANES - 1, 8, SIDE), F32),
        in_specs=[pl.BlockSpec(memory_space=SMEM)] + [pl.BlockSpec(memory_space=VMEM)] * (len(pieces) + 1),
        out_specs=pl.BlockSpec(memory_space=VMEM),
        name="update_probe",
    )(place, *pieces, probe.reshape(PLANES - 1, 32, 8, SIDE))


def gather_parts(slot, place, pieces):
    length = pieces[0].shape[0]

    def body(place, *refs):
        out = refs[-1]
        for step, piece in enumerate(refs[:-1]):
            start = lax.rem(place[slot] + 4 - step, 4) * length
            out[pl.ds(start, length)] = piece[...]

    return pl.pallas_call(
        body,
        out_shape=jax.ShapeDtypeStruct((4 * length,) + pieces[0].shape[1:], F32),
        in_specs=[pl.BlockSpec(memory_space=SMEM)] + [pl.BlockSpec(memory_space=VMEM)] * 4,
        out_specs=pl.BlockSpec(memory_space=VMEM),
        name="gather_parts",
    )(place, *pieces)


def join_halves(place, mine, other):
    def body(place, mine_ref, other_ref, out):
        core = place[2]
        for plane in range(PLANES - 1):
            for piece, start in ((mine_ref, core * 16), (other_ref, 16 - core * 16)):
                out[plane, pl.ds(start, 16)] = piece[:, plane]

    out = pl.pallas_call(
        body,
        out_shape=jax.ShapeDtypeStruct((PLANES - 1, 32, 8, SIDE), F32),
        in_specs=[pl.BlockSpec(memory_space=SMEM)] + [pl.BlockSpec(memory_space=VMEM)] * 2,
        out_specs=pl.BlockSpec(memory_space=VMEM),
        name="join_halves",
    )(place, mine, other)
    return out.reshape(MODES, 2, SIDE, SIDE)


def update_object(own, pieces, weight):
    def body(own_ref, *refs):
        weight_ref, out = refs[-2], refs[-1]
        scale = 1.0 / weight_ref[...]
        for part in range(2):
            block = own_ref[part]
            for piece in refs[:-2]:
                block = block + piece[part]
            out[part] = block * scale

    return pl.pallas_call(
        body,
        out_shape=jax.ShapeDtypeStruct((2, SIDE, SIDE), F32),
        in_specs=[pl.BlockSpec(memory_space=VMEM)] * (len(pieces) + 2),
        out_specs=pl.BlockSpec(memory_space=VMEM),
        compiler_params=pltpu.CompilerParams(vmem_limit_bytes=32 * 1024 * 1024),
        name="update_object",
    )(own, *pieces, weight)


def shards(object_field, probe, amplitudes, positions, counts):
    row_id = lax.axis_index("gy")
    col_id = lax.axis_index("gx")
    core = row_id % 2
    x_at = row_id // 4
    y_at = (row_id // 2) % 2 * 2 + col_id // 8
    first = jnp.where(core == 0, x_at, y_at)
    second = jnp.where(core == 0, y_at, x_at)
    place = jnp.stack([row_id, col_id, core, first, second]).astype(jnp.int32)
    table = jnp.asarray(transform_tables())
    order = jnp.asarray(order_table())

    points = positions[0, 0]
    right_strip = shifted(object_field, "gx", -1)
    lower_strip = shifted(object_field, "gy", -1)
    points_left = shifted(points, "gx", 1)
    points_pair = shifted(jnp.concatenate([points, points_left], 0), "gy", 1)
    diagonal = shifted(right_strip, "gy", -1)
    amplitude, weight = prepare(
        place, counts, points, points_left, points_pair[:SLOTS], points_pair[SLOTS:],
        probe, amplitudes[0, 0], order,
    )
    core_grad, right_grad, lower_grad, corner_grad, other_half, half = visit_patterns(
        place, counts, points, object_field, right_strip, lower_strip, diagonal, probe, amplitude, table
    )

    half_in = send(other_half, core_pair())
    parts = scatter_sum(3, place, [half, half_in])
    arrived = [send(parts[step], first_ring(step)) for step in (1, 2, 3)]
    corner_step = shifted(corner_grad, "gy", 1)
    parts = scatter_sum(4, place, [parts[0]] + arrived)
    arrived = [send(parts[step], second_ring(step)) for step in (1, 2, 3)]
    from_above = shifted(lower_grad, "gy", 1)
    block = plain_sum([parts[0]] + arrived)
    block = plain_sum([block, send(block, depth_pair())])
    chunk = update_probe(place, [block] + [send(block, depth_ring(step)) for step in (2, 4, 6)], probe)
    from_left = shifted(right_grad, "gx", 1)
    from_corner = shifted(corner_step, "gx", 1)
    chunk = gather_parts(4, place, [chunk] + [send(chunk, second_ring(step)) for step in (1, 2, 3)])
    chunk = gather_parts(3, place, [chunk] + [send(chunk, first_ring(step)) for step in (1, 2, 3)])
    new_probe = join_halves(place, chunk, send(chunk, core_pair()))
    new_object = update_object(
        object_field, [core_grad, from_left, from_above, from_corner], weight
    )
    return (new_object, new_probe)


def solution(mesh):
    in_specs = (
        P(None, "gy", "gx"),
        P(),
        P("gy", "gx", None, None, None),
        P("gy", "gx", None, None),
        P(),
    )
    out_specs = (P(None, "gy", "gx"), P())
    return jax.shard_map(shards, mesh=mesh, in_specs=in_specs, out_specs=out_specs, check_vma=False)
```

```python
import math

import jax
import jax.numpy as jnp
import numpy as np
from jax import lax
from jax.experimental import pallas as pl
from jax.experimental.pallas import tpu as pltpu
from jax.sharding import PartitionSpec as P

SIDE = 256
HALF = 128
MODES = 3
SLOTS = 4
PLANES = 2 * MODES + 1
AXES = ("gx", "gy")
SMALL = 16 * 1024 * 1024
LARGE = 60 * 1024 * 1024
VMEM = pltpu.VMEM
SMEM = pltpu.SMEM
F32 = jnp.float32
BF16 = jnp.bfloat16


def flat_index(x, y, z, core):
    return ((y % 2) * 8 + z) * 16 + x * 4 + (y // 2) * 2 + core


def routes(move):
    pairs = []
    for x in range(4):
        for y in range(4):
            for z in range(8):
                for core in range(2):
                    tx, ty, tz, tc = move(x, y, z, core)
                    pairs.append((flat_index(x, y, z, core), flat_index(tx % 4, ty % 4, tz % 8, tc % 2)))
    return pairs


def first_ring(step):
    return routes(lambda x, y, z, c: (x + step, y, z, c) if c == 0 else (x, y + step, z, c))


def second_ring(step):
    return routes(lambda x, y, z, c: (x, y + step, z, c) if c == 0 else (x + step, y, z, c))


def depth_ring(step):
    return routes(lambda x, y, z, c: (x, y, z + step, c))


def depth_pair():
    return routes(lambda x, y, z, c: (x, y, z ^ 1, c))


def core_pair():
    return routes(lambda x, y, z, c: (x, y, z, 1 - c))


def send(value, pairs):
    return lax.ppermute(value, AXES, pairs)


def shifted(value, axis, steps):
    count = lax.axis_size(axis)
    return lax.ppermute(value, axis, [(source, (source + steps) % count) for source in range(count)])


def split_table(matrix):
    high = matrix.astype(np.float32).astype(jnp.bfloat16)
    low = (matrix - high.astype(np.float64)).astype(jnp.bfloat16)
    return high, low


def transform_tables():
    n = np.arange(HALF)[:, None].astype(np.int64)
    k = np.arange(HALF)[None, :].astype(np.int64)
    tables = []
    for odd in (0, 1):
        angle = (n * (2 * k + odd) % SIDE) * (-2.0 * math.pi / SIDE)
        cos, sin = np.cos(angle) / 16.0, np.sin(angle) / 16.0
        right = np.block([[cos, sin], [-sin, cos]])
        for matrix in (right, right.T):
            tables.extend(split_table(matrix))
    return np.stack(tables)


def order_table():
    table = np.zeros((SIDE, SIDE), np.float32)
    order = np.concatenate([np.arange(0, SIDE, 2), np.arange(1, SIDE, 2)])
    table[order, np.arange(SIDE)] = 1.0
    return table.astype(jnp.bfloat16)


def split(value):
    high = value.astype(BF16)
    low = (value - high.astype(F32)).astype(BF16)
    return high, low


def dot(left, right):
    return jnp.dot(left, right, preferred_element_type=F32)


def apply_right(value, table, which):
    high, low = split(value)
    return dot(low, table[which]) + dot(high, table[which + 1]) + dot(high, table[which])


def apply_left(table, which, value):
    high, low = split(value)
    return dot(table[which], low) + dot(table[which + 1], high) + dot(table[which], high)


def lanes(*parts):
    return jnp.concatenate(parts, axis=1)


def rows(*parts):
    return jnp.concatenate(parts, axis=0)


def sort_kernel(amplitude, order, amp_out, measured, sems):
    loads = [
        pltpu.make_async_copy(
            amplitude.at[:, :, pl.ds(block * HALF, HALF)], measured.at[:, block], sems.at[block]
        )
        for block in range(2)
    ]
    for load in loads:
        load.start()
    for load in loads:
        load.wait()
    for item in range(SLOTS):
        sorted_rows = lanes(
            *[
                rows(*[measured[item, block, pl.ds(odd, HALF, stride=2), :] for odd in range(2)])
                for block in range(2)
            ]
        )
        high, rest = split(sorted_rows)
        rest32 = sorted_rows - high.astype(F32)
        middle, low = split(rest32)
        amp_out[item] = dot(high, order[...]) + (dot(middle, order[...]) + dot(low, order[...]))


def sort_amplitude(amplitude, order):
    return pl.pallas_call(
        sort_kernel,
        out_shape=jax.ShapeDtypeStruct((SLOTS, SIDE, SIDE), F32),
        in_specs=[pl.BlockSpec(memory_space=pl.ANY), pl.BlockSpec(memory_space=VMEM)],
        out_specs=pl.BlockSpec(memory_space=VMEM),
        scratch_shapes=[VMEM((SLOTS, 2, SIDE, HALF), F32), pltpu.SemaphoreType.DMA((2,))],
        compiler_params=pltpu.CompilerParams(vmem_limit_bytes=LARGE),
        cost_estimate=pl.CostEstimate(flops=2_000_000_000, bytes_accessed=4_000_000, transcendentals=0),
        name="sort_amplitude",
    )(amplitude, order)


def cover_kernel(place, counts, own, left, above, corner, probe, weight_out, doubled):
    coverage = probe[0, 0] * probe[0, 0]
    for mode in range(MODES):
        for part in range(2):
            if mode or part:
                coverage = coverage + probe[mode, part] * probe[mode, part]
    for block in range(2):
        for start in (0, SIDE):
            doubled[block, pl.ds(start, SIDE), :] = coverage[:, block * HALF : (block + 1) * HALF]
    row_id = place[0]
    col_id = place[1]
    row_iota = lax.broadcasted_iota(jnp.int32, (SIDE, SIDE), 0)
    lane_iota = lax.broadcasted_iota(jnp.int32, (SIDE, SIDE), 1)
    weight_out[...] = jnp.ones((SIDE, SIDE), F32)
    for up, back, points in ((0, 0, own), (0, 1, left), (1, 0, above), (1, 1, corner)):
        tile_row = row_id - up
        tile_col = col_id - back
        inside = jnp.logical_and(tile_row >= 0, tile_col >= 0)
        count = jnp.where(inside, counts[jnp.maximum(tile_row, 0), jnp.maximum(tile_col, 0)], 0)

        def visit(item, carry, points=points, tile_row=tile_row, tile_col=tile_col, up=up, back=back):
            row_at = points[item, 0] - tile_row * SIDE
            col_at = points[item, 1] - tile_col * SIDE
            window = pl.ds(SIDE - row_at, SIDE)
            moved = pltpu.roll(lanes(doubled[0, window, :], doubled[1, window, :]), col_at, 1)
            row_ok = row_iota < row_at if up else row_iota >= row_at
            col_ok = lane_iota < col_at if back else lane_iota >= col_at
            weight_out[...] += jnp.where(jnp.logical_and(row_ok, col_ok), moved, 0.0)
            return carry

        lax.fori_loop(0, count, visit, 0)


def cover(place, counts, own, left, above, corner, probe):
    return pl.pallas_call(
        cover_kernel,
        out_shape=jax.ShapeDtypeStruct((SIDE, SIDE), F32),
        in_specs=[pl.BlockSpec(memory_space=SMEM)] * 6 + [pl.BlockSpec(memory_space=VMEM)],
        out_specs=pl.BlockSpec(memory_space=VMEM),
        scratch_shapes=[VMEM((2, 2 * SIDE, HALF), F32)],
        compiler_params=pltpu.CompilerParams(vmem_limit_bytes=LARGE),
        cost_estimate=pl.CostEstimate(flops=2_000_000_000, bytes_accessed=4_000_000, transcendentals=0),
        name="cover",
    )(place, counts, own, left, above, corner, probe)


def pattern_kernel(
    place, counts, points, own, right, lower, corner, probe_in, amplitude_in, table_in,
    core_out, right_out, lower_out, send_out, keep_out,
    field, target, total, spectrum, probe, amplitude, table, sems,
):
    row_id = place[0]
    col_id = place[1]
    core = place[2]
    loads = []
    for piece, up, back in ((own, 0, 0), (right, 0, 1), (lower, 1, 0), (corner, 1, 1)):
        for block in range(2):
            loads.append(
                pltpu.make_async_copy(
                    piece.at[:, :, pl.ds(block * HALF, HALF)],
                    field.at[:, 2 * back + block, pl.ds(up * SIDE, SIDE), :],
                    sems.at[len(loads)],
                )
            )
    for source, dest in ((probe_in, probe), (table_in, table), (amplitude_in, amplitude)):
        loads.append(pltpu.make_async_copy(source, dest, sems.at[len(loads)]))
    for load in loads:
        load.start()
    target[...] = jnp.zeros_like(target)
    total[...] = jnp.zeros_like(total)
    for load in loads:
        load.wait()
    lane_iota = lax.broadcasted_iota(jnp.int32, (SIDE, SIDE), 1)

    def visit(item, carry):
        row_at = points[item, 0] - row_id * SIDE
        col_at = points[item, 1] - col_id * SIDE
        in_left = lane_iota >= col_at
        rest = jnp.where(col_at == 0, 0, SIDE - col_at)

        def cut(part):
            window = pl.ds(row_at, SIDE)
            first = lanes(field[part, 0, window, :], field[part, 1, window, :])
            second = lanes(field[part, 2, window, :], field[part, 3, window, :])
            return pltpu.roll(jnp.where(in_left, first, second), rest, 1)

        object_real = cut(0)
        object_imag = cut(1)
        density = object_real * object_real + object_imag * object_imag
        total[:, PLANES - 1] += density.reshape(32, 8, SIDE)

        even_sum = jnp.zeros((HALF, SIDE), F32)
        odd_sum = jnp.zeros((HALF, SIDE), F32)
        for mode in range(MODES):
            probe_real = probe[mode, 0]
            probe_imag = probe[mode, 1]
            real = probe_real * object_real - probe_imag * object_imag
            imag = probe_real * object_imag + probe_imag * object_real
            even = apply_right(
                lanes(real[:, :HALF] + real[:, HALF:], imag[:, :HALF] + imag[:, HALF:]), table, 0
            )
            odd = apply_right(
                lanes(real[:, :HALF] - real[:, HALF:], imag[:, :HALF] - imag[:, HALF:]), table, 4
            )
            real = lanes(even[:, :HALF], odd[:, :HALF])
            imag = lanes(even[:, HALF:], odd[:, HALF:])
            even = apply_left(table, 2, rows(real[:HALF] + real[HALF:], imag[:HALF] + imag[HALF:]))
            odd = apply_left(table, 6, rows(real[:HALF] - real[HALF:], imag[:HALF] - imag[HALF:]))
            spectrum[mode, 0] = even
            spectrum[mode, 1] = odd
            even_sum += even[:HALF] * even[:HALF] + even[HALF:] * even[HALF:]
            odd_sum += odd[:HALF] * odd[:HALF] + odd[HALF:] * odd[HALF:]
        even_factor = amplitude[item, :HALF] / jnp.maximum(jnp.sqrt(even_sum), 0.5)
        odd_factor = amplitude[item, HALF:] / jnp.maximum(jnp.sqrt(odd_sum), 0.5)
        even_factor = rows(even_factor, even_factor)
        odd_factor = rows(odd_factor, odd_factor)
        grad_real = jnp.zeros((SIDE, SIDE), F32)
        grad_imag = jnp.zeros((SIDE, SIDE), F32)
        for mode in range(MODES):
            even = apply_left(table, 0, spectrum[mode, 0] * even_factor)
            odd = apply_left(table, 4, spectrum[mode, 1] * odd_factor)
            high = even + odd
            low = even - odd
            real = rows(high[:HALF], low[:HALF])
            imag = rows(high[HALF:], low[HALF:])
            even = apply_right(lanes(real[:, :HALF], imag[:, :HALF]), table, 2)
            odd = apply_right(lanes(real[:, HALF:], imag[:, HALF:]), table, 6)
            high = even + odd
            low = even - odd
            real = lanes(high[:, :HALF], low[:, :HALF])
            imag = lanes(high[:, HALF:], low[:, HALF:])
            probe_real = probe[mode, 0]
            probe_imag = probe[mode, 1]
            grad_real += probe_real * real + probe_imag * imag
            grad_imag += probe_real * imag - probe_imag * real
            total[:, 2 * mode] += (object_real * real + object_imag * imag).reshape(32, 8, SIDE)
            total[:, 2 * mode + 1] += (object_real * imag - object_imag * real).reshape(32, 8, SIDE)
        for part, grad in ((0, grad_real), (1, grad_imag)):
            moved = pltpu.roll(grad, col_at, 1)
            first = jnp.where(in_left, moved, 0.0)
            second = jnp.where(in_left, 0.0, moved)
            window = pl.ds(row_at, SIDE)
            for block, piece in enumerate((first[:, :HALF], first[:, HALF:], second[:, :HALF], second[:, HALF:])):
                target[part, block, window, :] += piece
        return carry

    lax.fori_loop(0, counts[row_id, col_id], visit, 0)
    stores = [
        pltpu.make_async_copy(total.at[pl.ds((1 - core) * 16, 16)], send_out, sems.at[0]),
        pltpu.make_async_copy(total.at[pl.ds(core * 16, 16)], keep_out, sems.at[1]),
    ]
    for piece, up, tall, back in ((core_out, 0, 1, 0), (right_out, 0, 2, 1), (lower_out, 1, 1, 0)):
        for block in range(2):
            stores.append(
                pltpu.make_async_copy(
                    target.at[:, 2 * back + block, pl.ds(up * SIDE, tall * SIDE), :],
                    piece.at[:, :, pl.ds(block * HALF, HALF)],
                    sems.at[len(stores)],
                )
            )
    for store in stores:
        store.start()
    for store in stores:
        store.wait()


def visit_patterns(place, counts, points, own, right, lower, corner, probe, amplitude, table):
    tile = jax.ShapeDtypeStruct((2, SIDE, SIDE), F32)
    tall = jax.ShapeDtypeStruct((2, 2 * SIDE, SIDE), F32)
    part = jax.ShapeDtypeStruct((16, PLANES, 8, SIDE), F32)
    return pl.pallas_call(
        pattern_kernel,
        out_shape=(tile, tall, tile, part, part),
        in_specs=[pl.BlockSpec(memory_space=SMEM)] * 3 + [pl.BlockSpec(memory_space=pl.ANY)] * 7,
        out_specs=(pl.BlockSpec(memory_space=pl.ANY),) * 5,
        scratch_shapes=[
            VMEM((2, 4, 2 * SIDE, HALF), F32),
            VMEM((2, 4, 2 * SIDE, HALF), F32),
            VMEM((32, PLANES, 8, SIDE), F32),
            VMEM((MODES, 2, SIDE, SIDE), F32),
            VMEM(probe.shape, F32),
            VMEM(amplitude.shape, F32),
            VMEM(table.shape, BF16),
            pltpu.SemaphoreType.DMA((11,)),
        ],
        compiler_params=pltpu.CompilerParams(vmem_limit_bytes=LARGE),
        cost_estimate=pl.CostEstimate(flops=10_000_000_000, bytes_accessed=10_000_000, transcendentals=0),
        name="patterns",
    )(place, counts, points, own, right, lower, corner, probe, amplitude, table)


def small_call(body, name, out_shape, operands, scalars=0, unread=0, **options):
    held = len(operands) - scalars - unread
    out_specs = jax.tree.map(lambda _: pl.BlockSpec(memory_space=VMEM), out_shape)
    return pl.pallas_call(
        body,
        out_shape=out_shape,
        in_specs=[pl.BlockSpec(memory_space=SMEM)] * scalars
        + [pl.BlockSpec(memory_space=VMEM)] * held
        + [pl.BlockSpec(memory_space=pl.ANY)] * unread,
        out_specs=out_specs,
        compiler_params=pltpu.CompilerParams(vmem_limit_bytes=SMALL),
        name=name,
        **options,
    )(*operands)


def scatter_sum(slot, place, pieces):
    length = pieces[0].shape[0] // 4
    shape = (length,) + pieces[0].shape[1:]
    number = len(pieces)

    def body(place, *refs):
        outs = refs[-4:]
        for step in range(4):
            start = lax.rem(place[slot] + step, 4) * length
            block = refs[0][pl.ds(start, length)]
            for piece in refs[1:number]:
                block = block + piece[pl.ds(start, length)]
            outs[step][...] = block

    return small_call(body, "scatter_sum", (jax.ShapeDtypeStruct(shape, F32),) * 4, (place, *pieces), scalars=1)


def plain_sum(pieces):
    def body(*refs):
        block = refs[0][...]
        for piece in refs[1:-1]:
            block = block + piece[...]
        refs[-1][...] = block

    return small_call(body, "plain_sum", jax.ShapeDtypeStruct(pieces[0].shape, F32), pieces)


def update_probe(pieces, old):
    def body(*refs):
        old_ref, out = refs[-2:]
        block = refs[0][0]
        for piece in refs[1:-2]:
            block = block + piece[0]
        scale = 1.0 / (block[PLANES - 1] + 1.0)
        for plane in range(PLANES - 1):
            out[0, plane] = (old_ref[0, plane] + block[plane]) * scale

    return small_call(body, "update_probe", jax.ShapeDtypeStruct(old.shape, F32), (*pieces, old))


def own_rows(place, probe):
    def body(place, probe_ref, out):
        group = place[2] * 16 + place[3] * 4 + place[4]
        for plane in range(PLANES - 1):
            out[0, plane] = probe_ref[plane, group]

    return pl.pallas_call(
        body,
        out_shape=jax.ShapeDtypeStruct((1, PLANES - 1, 8, SIDE), F32),
        in_specs=[pl.BlockSpec(memory_space=SMEM), pl.BlockSpec(memory_space=VMEM)],
        out_specs=pl.BlockSpec(memory_space=VMEM),
        compiler_params=pltpu.CompilerParams(vmem_limit_bytes=LARGE),
        name="own_rows",
    )(place, probe.reshape(PLANES - 1, 32, 8, SIDE))


def gather_parts(pieces):
    length = pieces[0].shape[0]

    def body(*refs):
        for step, piece in enumerate(refs[:-1]):
            refs[-1][pl.ds(step * length, length)] = piece[...]

    shape = (4 * length,) + pieces[0].shape[1:]
    return small_call(body, "gather_parts", jax.ShapeDtypeStruct(shape, F32), pieces)


def join_halves(place, mine, other):
    def body(place, mine_ref, other_ref, out, sem):
        core, first, second = place[2], place[3], place[4]
        copies = []
        for piece, half, outer, inner in (
            (mine_ref, core, first, second), (other_ref, 1 - core, second, first)
        ):
            for one in range(4):
                for two in range(4):
                    group = half * 16 + lax.rem(outer + 4 - one, 4) * 4 + lax.rem(inner + 4 - two, 4)
                    copies.append(
                        pltpu.make_async_copy(piece.at[one * 4 + two], out.at[:, group], sem.at[len(copies)])
                    )
        for copy in copies:
            copy.start()
        for copy in copies:
            copy.wait()

    out = pl.pallas_call(
        body,
        out_shape=jax.ShapeDtypeStruct((PLANES - 1, 32, 8, SIDE), F32),
        in_specs=[pl.BlockSpec(memory_space=SMEM)] + [pl.BlockSpec(memory_space=pl.ANY)] * 2,
        out_specs=pl.BlockSpec(memory_space=pl.ANY),
        scratch_shapes=[pltpu.SemaphoreType.DMA((32,))],
        compiler_params=pltpu.CompilerParams(vmem_limit_bytes=SMALL),
        name="join_halves",
    )(place, mine, other)
    return out.reshape(MODES, 2, SIDE, SIDE)


def add_corner(lower, side, after):
    def body(lower_ref, side_ref, after_ref, out):
        out[...] = lower_ref[...] + side_ref[:, SIDE:, :]

    return small_call(
        body, "add_corner", jax.ShapeDtypeStruct(lower.shape, F32), (lower, side, after), unread=1
    )


def update_object(own, core, side, above, weight, after):
    def body(own_ref, core_ref, side_ref, above_ref, weight_ref, after_ref, out):
        scale = 1.0 / weight_ref[...]
        for part in range(2):
            block = own_ref[part] + core_ref[part]
            out[part] = (block + side_ref[part, :SIDE, :] + above_ref[part]) * scale

    return small_call(
        body, "update_object", jax.ShapeDtypeStruct(own.shape, F32),
        (own, core, side, above, weight, after), unread=1,
    )


def shards(object_field, probe, amplitudes, positions, counts):
    row_id = lax.axis_index("gy")
    col_id = lax.axis_index("gx")
    core = row_id % 2
    x_at = row_id // 4
    y_at = (row_id // 2) % 2 * 2 + col_id // 8
    first = jnp.where(core == 0, x_at, y_at)
    second = jnp.where(core == 0, y_at, x_at)
    place = jnp.stack([row_id, col_id, core, first, second]).astype(jnp.int32)
    table = jnp.asarray(transform_tables())
    order = jnp.asarray(order_table())

    points = positions[0, 0]
    right_strip = shifted(object_field, "gx", -1)
    lower_strip = shifted(object_field, "gy", -1)
    points_left = shifted(points, "gx", 1)
    amplitude = sort_amplitude(amplitudes[0, 0], order)
    old_rows = own_rows(place, probe)
    points_pair = shifted(jnp.concatenate([points, points_left], 0), "gy", 1)
    diagonal = shifted(right_strip, "gy", -1)
    weight = cover(place, counts, points, points_left, points_pair[:SLOTS], points_pair[SLOTS:], probe)
    core_grad, side_grad, lower_grad, other_half, half = visit_patterns(
        place, counts, points, object_field, right_strip, lower_strip, diagonal, probe, amplitude, table
    )

    half_in = send(other_half, core_pair())
    from_left = shifted(side_grad, "gx", 1)
    parts = scatter_sum(3, place, [half, half_in])
    arrived = [send(parts[step], first_ring(step)) for step in (1, 2, 3)]
    parts = scatter_sum(4, place, [parts[0]] + arrived)
    arrived = [send(parts[step], second_ring(step)) for step in (1, 2, 3)]
    block = plain_sum([parts[0]] + arrived)
    from_above = shifted(add_corner(lower_grad, from_left, block), "gy", 1)
    block = plain_sum([block, send(block, depth_pair())])
    chunk = update_probe([block] + [send(block, depth_ring(step)) for step in (2, 4, 6)], old_rows)
    chunk = gather_parts([chunk] + [send(chunk, second_ring(step)) for step in (1, 2, 3)])
    new_object = update_object(object_field, core_grad, from_left, from_above, weight, chunk)
    chunk = gather_parts([chunk] + [send(chunk, first_ring(step)) for step in (1, 2, 3)])
    new_probe = join_halves(place, chunk, send(chunk, core_pair()))
    return (new_object, new_probe)


def solution(mesh):
    in_specs = (
        P(None, "gy", "gx"),
        P(),
        P("gy", "gx", None, None, None),
        P("gy", "gx", None, None),
        P(),
    )
    out_specs = (P(None, "gy", "gx"), P())
    return jax.shard_map(shards, mesh=mesh, in_specs=in_specs, out_specs=out_specs, check_vma=False)
```

```python
import math

import jax
import jax.numpy as jnp
import numpy as np
from jax import lax
from jax.experimental import pallas as pl
from jax.experimental.pallas import tpu as pltpu
from jax.sharding import PartitionSpec as P

SIDE = 256
HALF = 128
MODES = 3
SLOTS = 4
PLANES = 2 * MODES + 1
AXES = ("gx", "gy")
SMALL = 16 * 1024 * 1024
LARGE = 40 * 1024 * 1024
VMEM = pltpu.VMEM
SMEM = pltpu.SMEM
F32 = jnp.float32
BF16 = jnp.bfloat16


def flat_index(x, y, z, core):
    return ((y % 2) * 8 + z) * 16 + x * 4 + (y // 2) * 2 + core


def routes(move):
    pairs = []
    for x in range(4):
        for y in range(4):
            for z in range(8):
                for core in range(2):
                    tx, ty, tz, tc = move(x, y, z, core)
                    pairs.append((flat_index(x, y, z, core), flat_index(tx % 4, ty % 4, tz % 8, tc % 2)))
    return pairs


def x_ring(step):
    return routes(lambda x, y, z, c: (x + step, y, z, c))


def y_ring(step):
    return routes(lambda x, y, z, c: (x, y + step, z, c))


def depth_ring(step):
    return routes(lambda x, y, z, c: (x, y, z + step, c))


def depth_pair():
    return routes(lambda x, y, z, c: (x, y, z ^ 1, c))


def core_pair():
    return routes(lambda x, y, z, c: (x, y, z, 1 - c))


def plane_groups():
    return [
        [flat_index(x, y, z, core) for x in range(4) for y in range(4)] for z in range(8) for core in range(2)
    ]


def swap_in_plane(value):
    return lax.all_to_all(value, AXES, split_axis=0, concat_axis=0, tiled=True, axis_index_groups=plane_groups())


def send(value, pairs):
    return lax.ppermute(value, AXES, pairs)


def shifted(value, axis, steps):
    count = lax.axis_size(axis)
    return lax.ppermute(value, axis, [(source, (source + steps) % count) for source in range(count)])


def split_table(matrix):
    high = matrix.astype(np.float32).astype(jnp.bfloat16)
    low = (matrix - high.astype(np.float64)).astype(jnp.bfloat16)
    return high, low


def transform_tables():
    n = np.arange(HALF)[:, None].astype(np.int64)
    k = np.arange(HALF)[None, :].astype(np.int64)
    tables = []
    for odd in (0, 1):
        angle = (n * (2 * k + odd) % SIDE) * (-2.0 * math.pi / SIDE)
        cos, sin = np.cos(angle) / 16.0, np.sin(angle) / 16.0
        right = np.block([[cos, sin], [-sin, cos]])
        for matrix in (right, right.T):
            tables.extend(split_table(matrix))
    return np.stack(tables)


def order_table():
    table = np.zeros((SIDE, SIDE), np.float32)
    order = np.concatenate([np.arange(0, SIDE, 2), np.arange(1, SIDE, 2)])
    table[order, np.arange(SIDE)] = 1.0
    return table.astype(jnp.bfloat16)


def split(value):
    high = value.astype(BF16)
    low = (value - high.astype(F32)).astype(BF16)
    return high, low


def dot(left, right):
    return jnp.dot(left, right, preferred_element_type=F32)


def apply_right(value, table, which):
    high, low = split(value)
    return dot(low, table[which]) + dot(high, table[which + 1]) + dot(high, table[which])


def apply_left(table, which, value):
    high, low = split(value)
    return dot(table[which], low) + dot(table[which + 1], high) + dot(table[which], high)


def lanes(*parts):
    return jnp.concatenate(parts, axis=1)


def rows(*parts):
    return jnp.concatenate(parts, axis=0)


def sort_kernel(amplitude, order, amp_out, measured, sems):
    loads = [
        pltpu.make_async_copy(
            amplitude.at[:, :, pl.ds(block * HALF, HALF)], measured.at[:, block], sems.at[block]
        )
        for block in range(2)
    ]
    for load in loads:
        load.start()
    for load in loads:
        load.wait()
    for item in range(SLOTS):
        sorted_rows = lanes(
            *[
                rows(*[measured[item, block, pl.ds(odd, HALF, stride=2), :] for odd in range(2)])
                for block in range(2)
            ]
        )
        high, rest = split(sorted_rows)
        rest32 = sorted_rows - high.astype(F32)
        middle, low = split(rest32)
        amp_out[item] = dot(high, order[...]) + (dot(middle, order[...]) + dot(low, order[...]))


def sort_amplitude(amplitude, order):
    return pl.pallas_call(
        sort_kernel,
        out_shape=jax.ShapeDtypeStruct((SLOTS, SIDE, SIDE), F32),
        in_specs=[pl.BlockSpec(memory_space=pl.ANY), pl.BlockSpec(memory_space=VMEM)],
        out_specs=pl.BlockSpec(memory_space=VMEM),
        scratch_shapes=[VMEM((SLOTS, 2, SIDE, HALF), F32), pltpu.SemaphoreType.DMA((2,))],
        compiler_params=pltpu.CompilerParams(vmem_limit_bytes=SMALL),
        cost_estimate=pl.CostEstimate(flops=2_000_000_000, bytes_accessed=4_000_000, transcendentals=0),
        name="sort_amplitude",
    )(amplitude, order)


def cover_kernel(place, counts, own, left, above, probe, weight_out, rows_out, doubled):
    start = pl.multiple_of((place[2] * 16 + place[3] * 4 + place[4]) * 8, 8)
    for mode in range(MODES):
        for part in range(2):
            rows_out[0, 2 * mode + part] = probe[mode, part, pl.ds(start, 8), :]
    coverage = probe[0, 0] * probe[0, 0]
    for mode in range(MODES):
        for part in range(2):
            if mode or part:
                coverage = coverage + probe[mode, part] * probe[mode, part]
    for block in range(2):
        for start in (0, SIDE):
            doubled[block, pl.ds(start, SIDE), :] = coverage[:, block * HALF : (block + 1) * HALF]
    row_id = place[0]
    col_id = place[1]
    row_iota = lax.broadcasted_iota(jnp.int32, (SIDE, SIDE), 0)
    lane_iota = lax.broadcasted_iota(jnp.int32, (SIDE, SIDE), 1)
    weight_out[...] = jnp.ones((SIDE, SIDE), F32)
    for up, back, points, skip in ((0, 0, own, 0), (0, 1, left, 0), (1, 0, above, 0), (1, 1, above, SLOTS)):
        tile_row = row_id - up
        tile_col = col_id - back
        inside = jnp.logical_and(tile_row >= 0, tile_col >= 0)
        count = jnp.where(inside, counts[jnp.maximum(tile_row, 0), jnp.maximum(tile_col, 0)], 0)

        def visit(item, carry, points=points, skip=skip, tile_row=tile_row, tile_col=tile_col, up=up, back=back):
            row_at = points[skip + item, 0] - tile_row * SIDE
            col_at = points[skip + item, 1] - tile_col * SIDE
            window = pl.ds(SIDE - row_at, SIDE)
            moved = pltpu.roll(lanes(doubled[0, window, :], doubled[1, window, :]), col_at, 1)
            row_ok = row_iota < row_at if up else row_iota >= row_at
            col_ok = lane_iota < col_at if back else lane_iota >= col_at
            weight_out[...] += jnp.where(jnp.logical_and(row_ok, col_ok), moved, 0.0)
            return carry

        lax.fori_loop(0, count, visit, 0)


def cover(place, counts, own, left, above, probe):
    return pl.pallas_call(
        cover_kernel,
        out_shape=(
            jax.ShapeDtypeStruct((SIDE, SIDE), F32),
            jax.ShapeDtypeStruct((1, PLANES - 1, 8, SIDE), F32),
        ),
        in_specs=[pl.BlockSpec(memory_space=SMEM)] * 5 + [pl.BlockSpec(memory_space=VMEM)],
        out_specs=(pl.BlockSpec(memory_space=VMEM),) * 2,
        scratch_shapes=[VMEM((2, 2 * SIDE, HALF), F32)],
        compiler_params=pltpu.CompilerParams(vmem_limit_bytes=SMALL),
        cost_estimate=pl.CostEstimate(flops=2_000_000_000, bytes_accessed=4_000_000, transcendentals=0),
        name="cover",
    )(place, counts, own, left, above, probe)


def pattern_kernel(
    place, counts, points, own, right, lower, corner, probe_in, amplitude_in, table_in, weight, old_rows,
    core_out, right_out, lower_out, send_out, keep_out,
    field, target, total, spectrum, probe, amplitude, table, sems,
):
    row_id = place[0]
    col_id = place[1]
    core = place[2]
    loads = []
    for piece, up, back in ((own, 0, 0), (right, 0, 1), (lower, 1, 0), (corner, 1, 1)):
        for block in range(2):
            loads.append(
                pltpu.make_async_copy(
                    piece.at[:, :, pl.ds(block * HALF, HALF)],
                    field.at[:, 2 * back + block, pl.ds(up * SIDE, SIDE), :],
                    sems.at[len(loads)],
                )
            )
    for source, dest in ((probe_in, probe), (table_in, table), (amplitude_in, amplitude)):
        loads.append(pltpu.make_async_copy(source, dest, sems.at[len(loads)]))
    for load in loads:
        load.start()
    target[...] = jnp.zeros_like(target)
    total[...] = jnp.zeros_like(total)
    for load in loads:
        load.wait()
    lane_iota = lax.broadcasted_iota(jnp.int32, (SIDE, SIDE), 1)

    def visit(item, carry):
        row_at = points[item, 0] - row_id * SIDE
        col_at = points[item, 1] - col_id * SIDE
        in_left = lane_iota >= col_at
        rest = jnp.where(col_at == 0, 0, SIDE - col_at)

        def cut(part):
            window = pl.ds(row_at, SIDE)
            first = lanes(field[part, 0, window, :], field[part, 1, window, :])
            second = lanes(field[part, 2, window, :], field[part, 3, window, :])
            return pltpu.roll(jnp.where(in_left, first, second), rest, 1)

        object_real = cut(0)
        object_imag = cut(1)
        density = object_real * object_real + object_imag * object_imag
        total[:, PLANES - 1] += density.reshape(32, 8, SIDE)

        even_sum = jnp.zeros((HALF, SIDE), F32)
        odd_sum = jnp.zeros((HALF, SIDE), F32)
        for mode in range(MODES):
            probe_real = probe[mode, 0]
            probe_imag = probe[mode, 1]
            real = probe_real * object_real - probe_imag * object_imag
            imag = probe_real * object_imag + probe_imag * object_real
            even = apply_right(
                lanes(real[:, :HALF] + real[:, HALF:], imag[:, :HALF] + imag[:, HALF:]), table, 0
            )
            odd = apply_right(
                lanes(real[:, :HALF] - real[:, HALF:], imag[:, :HALF] - imag[:, HALF:]), table, 4
            )
            real = lanes(even[:, :HALF], odd[:, :HALF])
            imag = lanes(even[:, HALF:], odd[:, HALF:])
            even = apply_left(table, 2, rows(real[:HALF] + real[HALF:], imag[:HALF] + imag[HALF:]))
            odd = apply_left(table, 6, rows(real[:HALF] - real[HALF:], imag[:HALF] - imag[HALF:]))
            spectrum[mode, 0] = even
            spectrum[mode, 1] = odd
            even_sum += even[:HALF] * even[:HALF] + even[HALF:] * even[HALF:]
            odd_sum += odd[:HALF] * odd[:HALF] + odd[HALF:] * odd[HALF:]
        even_factor = amplitude[item, :HALF] / jnp.maximum(jnp.sqrt(even_sum), 0.5)
        odd_factor = amplitude[item, HALF:] / jnp.maximum(jnp.sqrt(odd_sum), 0.5)
        even_factor = rows(even_factor, even_factor)
        odd_factor = rows(odd_factor, odd_factor)
        grad_real = jnp.zeros((SIDE, SIDE), F32)
        grad_imag = jnp.zeros((SIDE, SIDE), F32)
        for mode in range(MODES):
            even = apply_left(table, 0, spectrum[mode, 0] * even_factor)
            odd = apply_left(table, 4, spectrum[mode, 1] * odd_factor)
            high = even + odd
            low = even - odd
            real = rows(high[:HALF], low[:HALF])
            imag = rows(high[HALF:], low[HALF:])
            even = apply_right(lanes(real[:, :HALF], imag[:, :HALF]), table, 2)
            odd = apply_right(lanes(real[:, HALF:], imag[:, HALF:]), table, 6)
            high = even + odd
            low = even - odd
            real = lanes(high[:, :HALF], low[:, :HALF])
            imag = lanes(high[:, HALF:], low[:, HALF:])
            probe_real = probe[mode, 0]
            probe_imag = probe[mode, 1]
            grad_real += probe_real * real + probe_imag * imag
            grad_imag += probe_real * imag - probe_imag * real
            total[:, 2 * mode] += (object_real * real + object_imag * imag).reshape(32, 8, SIDE)
            total[:, 2 * mode + 1] += (object_real * imag - object_imag * real).reshape(32, 8, SIDE)
        for part, grad in ((0, grad_real), (1, grad_imag)):
            moved = pltpu.roll(grad, col_at, 1)
            first = jnp.where(in_left, moved, 0.0)
            second = jnp.where(in_left, 0.0, moved)
            window = pl.ds(row_at, SIDE)
            for block, piece in enumerate((first[:, :HALF], first[:, HALF:], second[:, :HALF], second[:, HALF:])):
                target[part, block, window, :] += piece
        return carry

    lax.fori_loop(0, counts[row_id, col_id], visit, 0)
    stores = [
        pltpu.make_async_copy(total.at[pl.ds((1 - core) * 16, 16)], send_out, sems.at[0]),
        pltpu.make_async_copy(total.at[pl.ds(core * 16, 16)], keep_out, sems.at[1]),
    ]
    for piece, up, tall, back in ((core_out, 0, 1, 0), (right_out, 0, 2, 1), (lower_out, 1, 1, 0)):
        for block in range(2):
            stores.append(
                pltpu.make_async_copy(
                    target.at[:, 2 * back + block, pl.ds(up * SIDE, tall * SIDE), :],
                    piece.at[:, :, pl.ds(block * HALF, HALF)],
                    sems.at[len(stores)],
                )
            )
    for store in stores:
        store.start()
    for store in stores:
        store.wait()


def visit_patterns(place, counts, points, own, right, lower, corner, probe, amplitude, table, *before):
    tile = jax.ShapeDtypeStruct((2, SIDE, SIDE), F32)
    tall = jax.ShapeDtypeStruct((2, 2 * SIDE, SIDE), F32)
    part = jax.ShapeDtypeStruct((16, PLANES, 8, SIDE), F32)
    return pl.pallas_call(
        pattern_kernel,
        out_shape=(tile, tall, tile, part, part),
        in_specs=[pl.BlockSpec(memory_space=SMEM)] * 3 + [pl.BlockSpec(memory_space=pl.ANY)] * 9,
        out_specs=(pl.BlockSpec(memory_space=pl.ANY),) * 5,
        scratch_shapes=[
            VMEM((2, 4, 2 * SIDE, HALF), F32),
            VMEM((2, 4, 2 * SIDE, HALF), F32),
            VMEM((32, PLANES, 8, SIDE), F32),
            VMEM((MODES, 2, SIDE, SIDE), F32),
            VMEM(probe.shape, F32),
            VMEM(amplitude.shape, F32),
            VMEM(table.shape, BF16),
            pltpu.SemaphoreType.DMA((11,)),
        ],
        compiler_params=pltpu.CompilerParams(vmem_limit_bytes=LARGE),
        cost_estimate=pl.CostEstimate(flops=10_000_000_000, bytes_accessed=10_000_000, transcendentals=0),
        name="patterns",
    )(place, counts, points, own, right, lower, corner, probe, amplitude, table, *before)


def small_call(body, name, out_shape, operands, scalars=0, unread=0, **options):
    held = len(operands) - scalars - unread
    out_specs = jax.tree.map(lambda _: pl.BlockSpec(memory_space=VMEM), out_shape)
    return pl.pallas_call(
        body,
        out_shape=out_shape,
        in_specs=[pl.BlockSpec(memory_space=SMEM)] * scalars
        + [pl.BlockSpec(memory_space=VMEM)] * held
        + [pl.BlockSpec(memory_space=pl.ANY)] * unread,
        out_specs=out_specs,
        compiler_params=pltpu.CompilerParams(vmem_limit_bytes=SMALL),
        name=name,
        **options,
    )(*operands)


def plain_sum(pieces, *before):
    number = len(pieces)

    def body(*refs):
        block = refs[0][...]
        for piece in refs[1:number]:
            block = block + piece[...]
        refs[-1][...] = block

    return small_call(
        body, "plain_sum", jax.ShapeDtypeStruct(pieces[0].shape, F32), (*pieces, *before), unread=len(before)
    )


def scatter_sum(slot, place, pieces):
    length = pieces[0].shape[0] // 4
    shape = (length,) + pieces[0].shape[1:]
    number = len(pieces)

    def body(place, *refs):
        outs = refs[-4:]
        for step in range(4):
            start = lax.rem(place[slot] + step, 4) * length
            block = refs[0][pl.ds(start, length)]
            for piece in refs[1:number]:
                block = block + piece[pl.ds(start, length)]
            outs[step][...] = block

    return small_call(body, "scatter_sum", (jax.ShapeDtypeStruct(shape, F32),) * 4, (place, *pieces), scalars=1)


def update_probe(pieces, old, *before):
    number = len(pieces)

    def body(*refs):
        old_ref, out = refs[number], refs[-1]
        block = refs[0][0]
        for piece in refs[1:number]:
            block = block + piece[0]
        scale = 1.0 / (block[PLANES - 1] + 1.0)
        for plane in range(PLANES - 1):
            new = (old_ref[0, plane] + block[plane]) * scale
            for copy in range(16):
                out[copy, plane] = new

    return small_call(
        body, "update_probe", jax.ShapeDtypeStruct((16,) + old.shape[1:], F32), (*pieces, old, *before),
        unread=len(before),
    )


def join_halves(place, mine, other):
    def body(place, mine_ref, other_ref, out, sem):
        core = place[2]
        copies = []
        for piece, half in ((mine_ref, core), (other_ref, 1 - core)):
            for plane in range(PLANES - 1):
                copies.append(
                    pltpu.make_async_copy(
                        piece.at[:, plane], out.at[plane, pl.ds(half * 16, 16)], sem.at[len(copies)]
                    )
                )
        for copy in copies:
            copy.start()
        for copy in copies:
            copy.wait()

    out = pl.pallas_call(
        body,
        out_shape=jax.ShapeDtypeStruct((PLANES - 1, 32, 8, SIDE), F32),
        in_specs=[pl.BlockSpec(memory_space=SMEM)] + [pl.BlockSpec(memory_space=pl.ANY)] * 2,
        out_specs=pl.BlockSpec(memory_space=pl.ANY),
        scratch_shapes=[pltpu.SemaphoreType.DMA((12,))],
        compiler_params=pltpu.CompilerParams(vmem_limit_bytes=SMALL),
        name="join_halves",
    )(place, mine, other)
    return out.reshape(MODES, 2, SIDE, SIDE)


def after(value, *events):
    def body(*refs):
        pass

    return pl.pallas_call(
        body,
        out_shape=jax.ShapeDtypeStruct(value.shape, value.dtype),
        in_specs=[pl.BlockSpec(memory_space=pl.ANY)] * (1 + len(events)),
        out_specs=pl.BlockSpec(memory_space=pl.ANY),
        input_output_aliases={0: 0},
        compiler_params=pltpu.CompilerParams(vmem_limit_bytes=SMALL),
        name="after",
    )(value, *events)


def add_corner(lower, left, *before):
    def body(lower_ref, left_ref, *refs):
        refs[-1][...] = lower_ref[...] + left_ref[:, SIDE:, :]

    return small_call(
        body, "add_corner", jax.ShapeDtypeStruct(lower.shape, F32), (lower, left, *before), unread=len(before)
    )


def update_object(own, core, left, above, weight):
    def body(own_ref, core_ref, left_ref, above_ref, weight_ref, out):
        scale = 1.0 / weight_ref[...]
        for part in range(2):
            block = own_ref[part] + core_ref[part]
            out[part] = (block + left_ref[part, :SIDE, :] + above_ref[part]) * scale

    return small_call(
        body, "update_object", jax.ShapeDtypeStruct(own.shape, F32), (own, core, left, above, weight)
    )


def shards(object_field, probe, amplitudes, positions, counts):
    row_id = lax.axis_index("gy")
    col_id = lax.axis_index("gx")
    core = row_id % 2
    x_at = row_id // 4
    y_at = (row_id // 2) % 2 * 2 + col_id // 8
    place = jnp.stack([row_id, col_id, core, x_at, y_at]).astype(jnp.int32)
    table = jnp.asarray(transform_tables())
    order = jnp.asarray(order_table())

    points = positions[0, 0]
    right_strip = shifted(object_field, "gx", -1)
    lower_strip = shifted(object_field, "gy", -1)
    points_left = shifted(points, "gx", 1)
    amplitude = sort_amplitude(amplitudes[0, 0], order)
    points_pair = shifted(jnp.concatenate([points, points_left], 0), "gy", 1)
    right_strip = after(right_strip, amplitude, points_pair, place)
    diagonal = shifted(right_strip, "gy", -1)
    weight, old_rows = cover(place, counts, points, points_left, points_pair, probe)
    core_grad, side_grad, lower_grad, other_half, half = visit_patterns(
        place, counts, points, object_field, right_strip, lower_strip, diagonal, probe, amplitude, table,
        weight, old_rows,
    )

    half_in = send(other_half, core_pair())
    from_left = shifted(side_grad, "gx", 1)
    parts = scatter_sum(3, place, [half, half_in])
    arrived = [send(parts[step], x_ring(step)) for step in (1, 2, 3)]
    parts = scatter_sum(4, place, [parts[0]] + arrived)
    arrived = [send(parts[step], y_ring(step)) for step in (1, 2, 3)]
    block = plain_sum([parts[0]] + arrived)
    from_above = shifted(add_corner(lower_grad, from_left, block), "gy", 1)
    block = plain_sum([block, send(block, depth_pair())])
    fours = [send(block, depth_ring(step)) for step in (2, 4, 6)]
    chunk = swap_in_plane(update_probe([block] + fours, old_rows, from_above))
    new_object = update_object(object_field, core_grad, from_left, from_above, weight)
    new_probe = join_halves(place, chunk, send(chunk, core_pair()))
    return (new_object, new_probe)


def solution(mesh):
    in_specs = (
        P(None, "gy", "gx"),
        P(),
        P("gy", "gx", None, None, None),
        P("gy", "gx", None, None),
        P(),
    )
    out_specs = (P(None, "gy", "gx"), P())
    return jax.shard_map(shards, mesh=mesh, in_specs=in_specs, out_specs=out_specs, check_vma=False)
```

```python
import math

import jax
import jax.numpy as jnp
import numpy as np
from jax import lax
from jax.experimental import pallas as pl
from jax.experimental.pallas import tpu as pltpu
from jax.sharding import PartitionSpec as P

SIDE = 256
HALF = 128
MODES = 3
SLOTS = 4
PLANES = 2 * MODES + 1
AXES = ("gx", "gy")
SMALL = 16 * 1024 * 1024
LARGE = 40 * 1024 * 1024
VMEM = pltpu.VMEM
SMEM = pltpu.SMEM
F32 = jnp.float32
BF16 = jnp.bfloat16


def flat_index(x, y, z, core):
    return ((y % 2) * 8 + z) * 16 + x * 4 + (y // 2) * 2 + core


def routes(move):
    pairs = []
    for x in range(4):
        for y in range(4):
            for z in range(8):
                for core in range(2):
                    tx, ty, tz, tc = move(x, y, z, core)
                    pairs.append((flat_index(x, y, z, core), flat_index(tx % 4, ty % 4, tz % 8, tc % 2)))
    return pairs


def x_ring(step):
    return routes(lambda x, y, z, c: (x + step, y, z, c))


def y_ring(step):
    return routes(lambda x, y, z, c: (x, y + step, z, c))


def depth_ring(step):
    return routes(lambda x, y, z, c: (x, y, z + step, c))


def depth_pair():
    return routes(lambda x, y, z, c: (x, y, z ^ 1, c))


def core_pair():
    return routes(lambda x, y, z, c: (x, y, z, 1 - c))


def plane_groups():
    return [
        [flat_index(x, y, z, core) for x in range(4) for y in range(4)] for z in range(8) for core in range(2)
    ]


def swap_in_plane(value):
    return lax.all_to_all(value, AXES, split_axis=0, concat_axis=0, tiled=True, axis_index_groups=plane_groups())


def send(value, pairs):
    return lax.ppermute(value, AXES, pairs)


def shifted(value, axis, steps):
    count = lax.axis_size(axis)
    return lax.ppermute(value, axis, [(source, (source + steps) % count) for source in range(count)])


def split_table(matrix):
    high = matrix.astype(np.float32).astype(jnp.bfloat16)
    low = (matrix - high.astype(np.float64)).astype(jnp.bfloat16)
    return high, low


def transform_tables():
    n = np.arange(HALF)[:, None].astype(np.int64)
    k = np.arange(HALF)[None, :].astype(np.int64)
    tables = []
    for odd in (0, 1):
        angle = (n * (2 * k + odd) % SIDE) * (-2.0 * math.pi / SIDE)
        cos, sin = np.cos(angle) / 16.0, np.sin(angle) / 16.0
        right = np.block([[cos, sin], [-sin, cos]])
        for matrix in (right, right.T):
            tables.extend(split_table(matrix))
    return np.stack(tables)


def order_table():
    table = np.zeros((SIDE, SIDE), np.float32)
    order = np.concatenate([np.arange(0, SIDE, 2), np.arange(1, SIDE, 2)])
    table[order, np.arange(SIDE)] = 1.0
    return table.astype(jnp.bfloat16)


def split(value):
    high = value.astype(BF16)
    low = (value - high.astype(F32)).astype(BF16)
    return high, low


def dot(left, right):
    return jnp.dot(left, right, preferred_element_type=F32)


STEP = 64
LAG = 6


def add_split(parts, even, odd):
    for index, value in enumerate((even, odd)):
        high, low = split(value)
        parts[2 * index].append(high)
        parts[2 * index + 1].append(low)


def run_staggered(chains):
    step = 0
    while chains:
        for index, chain in enumerate(list(chains)):
            if chain is not None and step >= index * LAG:
                if next(chain, "end") == "end":
                    chains[index] = None
        step += 1
        if all(chain is None for chain in chains):
            return


def lanes(*parts):
    return jnp.concatenate(parts, axis=1)


def rows(*parts):
    return jnp.concatenate(parts, axis=0)


def sort_kernel(amplitude, order, amp_out, measured, sems):
    loads = [
        pltpu.make_async_copy(
            amplitude.at[:, :, pl.ds(block * HALF, HALF)], measured.at[:, block], sems.at[block]
        )
        for block in range(2)
    ]
    for load in loads:
        load.start()
    for load in loads:
        load.wait()
    for item in range(SLOTS):
        sorted_rows = lanes(
            *[
                rows(*[measured[item, block, pl.ds(odd, HALF, stride=2), :] for odd in range(2)])
                for block in range(2)
            ]
        )
        high, rest = split(sorted_rows)
        rest32 = sorted_rows - high.astype(F32)
        middle, low = split(rest32)
        amp_out[item] = dot(high, order[...]) + (dot(middle, order[...]) + dot(low, order[...]))


def sort_amplitude(amplitude, order):
    return pl.pallas_call(
        sort_kernel,
        out_shape=jax.ShapeDtypeStruct((SLOTS, SIDE, SIDE), F32),
        in_specs=[pl.BlockSpec(memory_space=pl.ANY), pl.BlockSpec(memory_space=VMEM)],
        out_specs=pl.BlockSpec(memory_space=VMEM),
        scratch_shapes=[VMEM((SLOTS, 2, SIDE, HALF), F32), pltpu.SemaphoreType.DMA((2,))],
        compiler_params=pltpu.CompilerParams(vmem_limit_bytes=SMALL),
        cost_estimate=pl.CostEstimate(flops=2_000_000_000, bytes_accessed=4_000_000, transcendentals=0),
        name="sort_amplitude",
    )(amplitude, order)


def cover_kernel(place, counts, own, left, above, probe, weight_out, rows_out, doubled):
    start = pl.multiple_of((place[2] * 16 + place[3] * 4 + place[4]) * 8, 8)
    for mode in range(MODES):
        for part in range(2):
            rows_out[0, 2 * mode + part] = probe[mode, part, pl.ds(start, 8), :]
    coverage = probe[0, 0] * probe[0, 0]
    for mode in range(MODES):
        for part in range(2):
            if mode or part:
                coverage = coverage + probe[mode, part] * probe[mode, part]
    for block in range(2):
        for start in (0, SIDE):
            doubled[block, pl.ds(start, SIDE), :] = coverage[:, block * HALF : (block + 1) * HALF]
    row_id = place[0]
    col_id = place[1]
    row_iota = lax.broadcasted_iota(jnp.int32, (SIDE, SIDE), 0)
    lane_iota = lax.broadcasted_iota(jnp.int32, (SIDE, SIDE), 1)
    weight_out[...] = jnp.ones((SIDE, SIDE), F32)
    for up, back, points, skip in ((0, 0, own, 0), (0, 1, left, 0), (1, 0, above, 0), (1, 1, above, SLOTS)):
        tile_row = row_id - up
        tile_col = col_id - back
        inside = jnp.logical_and(tile_row >= 0, tile_col >= 0)
        count = jnp.where(inside, counts[jnp.maximum(tile_row, 0), jnp.maximum(tile_col, 0)], 0)

        def visit(item, carry, points=points, skip=skip, tile_row=tile_row, tile_col=tile_col, up=up, back=back):
            row_at = points[skip + item, 0] - tile_row * SIDE
            col_at = points[skip + item, 1] - tile_col * SIDE
            window = pl.ds(SIDE - row_at, SIDE)
            moved = pltpu.roll(lanes(doubled[0, window, :], doubled[1, window, :]), col_at, 1)
            row_ok = row_iota < row_at if up else row_iota >= row_at
            col_ok = lane_iota < col_at if back else lane_iota >= col_at
            weight_out[...] += jnp.where(jnp.logical_and(row_ok, col_ok), moved, 0.0)
            return carry

        lax.fori_loop(0, count, visit, 0)


def cover(place, counts, own, left, above, probe):
    return pl.pallas_call(
        cover_kernel,
        out_shape=(
            jax.ShapeDtypeStruct((SIDE, SIDE), F32),
            jax.ShapeDtypeStruct((1, PLANES - 1, 8, SIDE), F32),
        ),
        in_specs=[pl.BlockSpec(memory_space=SMEM)] * 5 + [pl.BlockSpec(memory_space=VMEM)],
        out_specs=(pl.BlockSpec(memory_space=VMEM),) * 2,
        scratch_shapes=[VMEM((2, 2 * SIDE, HALF), F32)],
        compiler_params=pltpu.CompilerParams(vmem_limit_bytes=SMALL),
        cost_estimate=pl.CostEstimate(flops=2_000_000_000, bytes_accessed=4_000_000, transcendentals=0),
        name="cover",
    )(place, counts, own, left, above, probe)


def pattern_kernel(
    place, counts, points, own, right_real, right_imag, lower, corner_real, corner_imag, probe_in, amplitude_in, table_in, weight, old_rows,
    core_out, right_out, lower_out, send_out, keep_out,
    field, target, total, spectrum, probe, amplitude, table, sems,
):
    row_id = place[0]
    col_id = place[1]
    core = place[2]
    loads = []
    for piece, part, length, up, back in (
        (own, 0, 2, 0, 0), (lower, 0, 2, 1, 0),
        (right_real, 0, 1, 0, 1), (right_imag, 1, 1, 0, 1),
        (corner_real, 0, 1, 1, 1), (corner_imag, 1, 1, 1, 1),
    ):
        for block in range(2):
            loads.append(
                pltpu.make_async_copy(
                    piece.at[:, :, pl.ds(block * HALF, HALF)],
                    field.at[pl.ds(part, length), 2 * back + block, pl.ds(up * SIDE, SIDE), :],
                    sems.at[len(loads)],
                )
            )
    for source, dest in ((probe_in, probe), (table_in, table), (amplitude_in, amplitude)):
        loads.append(pltpu.make_async_copy(source, dest, sems.at[len(loads)]))
    for load in loads:
        load.start()
    target[...] = jnp.zeros_like(target)
    total[...] = jnp.zeros_like(total)
    for load in loads:
        load.wait()
    lane_iota = lax.broadcasted_iota(jnp.int32, (SIDE, SIDE), 1)

    def visit(item, carry):
        row_at = points[item, 0] - row_id * SIDE
        col_at = points[item, 1] - col_id * SIDE
        in_left = lane_iota >= col_at
        rest = jnp.where(col_at == 0, 0, SIDE - col_at)

        def cut(part):
            window = pl.ds(row_at, SIDE)
            first = lanes(field[part, 0, window, :], field[part, 1, window, :])
            second = lanes(field[part, 2, window, :], field[part, 3, window, :])
            return pltpu.roll(jnp.where(in_left, first, second), rest, 1)

        object_real = cut(0)
        object_imag = cut(1)
        density = object_real * object_real + object_imag * object_imag
        total[:, PLANES - 1] += density.reshape(32, 8, SIDE)

        sums = {}

        def forward(mode):
            probe_real = probe[mode, 0]
            probe_imag = probe[mode, 1]
            parts = [[], [], [], []]
            for at in range(0, SIDE, STEP):
                cut_rows = slice(at, at + STEP)
                p_real, p_imag = probe_real[cut_rows], probe_imag[cut_rows]
                o_real, o_imag = object_real[cut_rows], object_imag[cut_rows]
                real = p_real * o_real - p_imag * o_imag
                imag = p_real * o_imag + p_imag * o_real
                both = lanes(real[:, :HALF], imag[:, :HALF]), lanes(real[:, HALF:], imag[:, HALF:])
                add_split(parts, both[0] + both[1], both[0] - both[1])
                yield
            high, low, odd_high, odd_low = [rows(*part) for part in parts]
            even = dot(lanes(low, high, high), rows(table[0], table[1], table[0]))
            yield
            odd = dot(lanes(odd_low, odd_high, odd_high), rows(table[4], table[5], table[4]))
            yield
            parts = [[], [], [], []]
            for lane in (slice(0, HALF), slice(HALF, SIDE)):
                for at in range(0, HALF, STEP // 2):
                    top, bottom = slice(at, at + STEP // 2), slice(HALF + at, HALF + at + STEP // 2)
                    first = lanes(even[top, lane], odd[top, lane])
                    second = lanes(even[bottom, lane], odd[bottom, lane])
                    add_split(parts, first + second, first - second)
                    yield
            high, low, odd_high, odd_low = [rows(*part) for part in parts]
            even = dot(lanes(table[2], table[3], table[2]), rows(low, high, high))
            yield
            odd = dot(lanes(table[6], table[7], table[6]), rows(odd_low, odd_high, odd_high))
            yield
            for index, values in enumerate((even, odd)):
                spectrum[mode, index] = values
                power = values[:HALF] * values[:HALF] + values[HALF:] * values[HALF:]
                sums[index] = sums[index] + power if index in sums else power
                yield

        run_staggered([forward(mode) for mode in range(MODES)])
        factors = []
        for index in range(2):
            factor = amplitude[item, index * HALF : index * HALF + HALF] * lax.rsqrt(jnp.maximum(sums[index], 0.25))
            factors.append(rows(factor, factor))
        grads = []

        def backward(mode):
            halves = []
            for index in range(2):
                parts = [[], []]
                for at in range(0, SIDE, STEP):
                    cut_rows = slice(at, at + STEP)
                    value = spectrum[mode, index, pl.ds(at, STEP), :] * factors[index][cut_rows]
                    high, low = split(value)
                    parts[0].append(high)
                    parts[1].append(low)
                    yield
                halves.append([rows(*part) for part in parts])
            (high, low), (odd_high, odd_low) = halves
            even = dot(lanes(table[0], table[1], table[0]), rows(low, high, high))
            yield
            odd = dot(lanes(table[4], table[5], table[4]), rows(odd_low, odd_high, odd_high))
            yield
            parts = [[], [], [], []]
            for sign in (1, -1):
                for at in range(0, HALF, STEP // 2):
                    real, imag = slice(at, at + STEP // 2), slice(HALF + at, HALF + at + STEP // 2)
                    if sign == 1:
                        first, second = even[real] + odd[real], even[imag] + odd[imag]
                    else:
                        first, second = even[real] - odd[real], even[imag] - odd[imag]
                    add_split(
                        parts, lanes(first[:, :HALF], second[:, :HALF]), lanes(first[:, HALF:], second[:, HALF:])
                    )
                    yield
            high, low, odd_high, odd_low = [rows(*part) for part in parts]
            even = dot(lanes(low, high, high), rows(table[2], table[3], table[2]))
            yield
            odd = dot(lanes(odd_low, odd_high, odd_high), rows(table[6], table[7], table[6]))
            yield
            pieces = []
            for at in range(0, SIDE, STEP):
                cut_rows = slice(at, at + STEP)
                first, second = even[cut_rows] + odd[cut_rows], even[cut_rows] - odd[cut_rows]
                real = lanes(first[:, :HALF], second[:, :HALF])
                imag = lanes(first[:, HALF:], second[:, HALF:])
                p_real, p_imag = probe[mode, 0, pl.ds(at, STEP), :], probe[mode, 1, pl.ds(at, STEP), :]
                o_real, o_imag = object_real[cut_rows], object_imag[cut_rows]
                pieces.append((p_real * real + p_imag * imag, p_real * imag - p_imag * real))
                groups = pl.ds(at // 8, STEP // 8)
                total[groups, 2 * mode] += (o_real * real + o_imag * imag).reshape(STEP // 8, 8, SIDE)
                total[groups, 2 * mode + 1] += (o_real * imag - o_imag * real).reshape(STEP // 8, 8, SIDE)
                yield
            grads.append([rows(*[piece[part] for piece in pieces]) for part in range(2)])

        run_staggered([backward(mode) for mode in range(MODES)])
        grad_real = grads[0][0] + grads[1][0] + grads[2][0]
        grad_imag = grads[0][1] + grads[1][1] + grads[2][1]
        for part, grad in ((0, grad_real), (1, grad_imag)):
            moved = pltpu.roll(grad, col_at, 1)
            first = jnp.where(in_left, moved, 0.0)
            second = jnp.where(in_left, 0.0, moved)
            window = pl.ds(row_at, SIDE)
            for block, piece in enumerate((first[:, :HALF], first[:, HALF:], second[:, :HALF], second[:, HALF:])):
                target[part, block, window, :] += piece
        return carry

    lax.fori_loop(0, counts[row_id, col_id], visit, 0)
    stores = [
        pltpu.make_async_copy(total.at[pl.ds((1 - core) * 16, 16)], send_out, sems.at[0]),
        pltpu.make_async_copy(total.at[pl.ds(core * 16, 16)], keep_out, sems.at[1]),
    ]
    for piece, up, tall, back in ((core_out, 0, 1, 0), (right_out, 0, 2, 1), (lower_out, 1, 1, 0)):
        for block in range(2):
            stores.append(
                pltpu.make_async_copy(
                    target.at[:, 2 * back + block, pl.ds(up * SIDE, tall * SIDE), :],
                    piece.at[:, :, pl.ds(block * HALF, HALF)],
                    sems.at[len(stores)],
                )
            )
    for store in stores:
        store.start()
    for store in stores:
        store.wait()


def visit_patterns(place, counts, points, own, right, lower, corner, probe, amplitude, table, *before):
    tile = jax.ShapeDtypeStruct((2, SIDE, SIDE), F32)
    tall = jax.ShapeDtypeStruct((2, 2 * SIDE, SIDE), F32)
    part = jax.ShapeDtypeStruct((16, PLANES, 8, SIDE), F32)
    return pl.pallas_call(
        pattern_kernel,
        out_shape=(tile, tall, tile, part, part),
        in_specs=[pl.BlockSpec(memory_space=SMEM)] * 3 + [pl.BlockSpec(memory_space=pl.ANY)] * 11,
        out_specs=(pl.BlockSpec(memory_space=pl.ANY),) * 5,
        scratch_shapes=[
            VMEM((2, 4, 2 * SIDE, HALF), F32),
            VMEM((2, 4, 2 * SIDE, HALF), F32),
            VMEM((32, PLANES, 8, SIDE), F32),
            VMEM((MODES, 2, SIDE, SIDE), F32),
            VMEM(probe.shape, F32),
            VMEM(amplitude.shape, F32),
            VMEM(table.shape, BF16),
            pltpu.SemaphoreType.DMA((15,)),
        ],
        compiler_params=pltpu.CompilerParams(vmem_limit_bytes=LARGE),
        cost_estimate=pl.CostEstimate(flops=10_000_000_000, bytes_accessed=10_000_000, transcendentals=0),
        name="patterns",
    )(place, counts, points, own, *right, lower, *corner, probe, amplitude, table, *before)


def small_call(body, name, out_shape, operands, scalars=0, unread=0, **options):
    held = len(operands) - scalars - unread
    out_specs = jax.tree.map(lambda _: pl.BlockSpec(memory_space=VMEM), out_shape)
    return pl.pallas_call(
        body,
        out_shape=out_shape,
        in_specs=[pl.BlockSpec(memory_space=SMEM)] * scalars
        + [pl.BlockSpec(memory_space=VMEM)] * held
        + [pl.BlockSpec(memory_space=pl.ANY)] * unread,
        out_specs=out_specs,
        compiler_params=pltpu.CompilerParams(vmem_limit_bytes=SMALL),
        name=name,
        **options,
    )(*operands)


def plain_sum(pieces, *before):
    number = len(pieces)

    def body(*refs):
        block = refs[0][...]
        for piece in refs[1:number]:
            block = block + piece[...]
        refs[-1][...] = block

    return small_call(
        body, "plain_sum", jax.ShapeDtypeStruct(pieces[0].shape, F32), (*pieces, *before), unread=len(before)
    )


def scatter_sum(slot, place, pieces):
    length = pieces[0].shape[0] // 4
    shape = (length,) + pieces[0].shape[1:]
    number = len(pieces)

    def body(place, *refs):
        outs = refs[-4:]
        for step in range(4):
            start = lax.rem(place[slot] + step, 4) * length
            block = refs[0][pl.ds(start, length)]
            for piece in refs[1:number]:
                block = block + piece[pl.ds(start, length)]
            outs[step][...] = block

    return small_call(body, "scatter_sum", (jax.ShapeDtypeStruct(shape, F32),) * 4, (place, *pieces), scalars=1)


def update_probe(pieces, old, *before):
    number = len(pieces)

    def body(*refs):
        old_ref, out = refs[number], refs[-1]
        block = refs[0][0]
        for piece in refs[1:number]:
            block = block + piece[0]
        scale = 1.0 / (block[PLANES - 1] + 1.0)
        for plane in range(PLANES - 1):
            new = (old_ref[0, plane] + block[plane]) * scale
            for copy in range(16):
                out[copy, plane] = new

    return small_call(
        body, "update_probe", jax.ShapeDtypeStruct((16,) + old.shape[1:], F32), (*pieces, old, *before),
        unread=len(before),
    )


def join_halves(place, mine, other):
    def body(place, mine_ref, other_ref, out, sem):
        core = place[2]
        copies = []
        for piece, half in ((mine_ref, core), (other_ref, 1 - core)):
            for plane in range(PLANES - 1):
                copies.append(
                    pltpu.make_async_copy(
                        piece.at[:, plane], out.at[plane, pl.ds(half * 16, 16)], sem.at[len(copies)]
                    )
                )
        for copy in copies:
            copy.start()
        for copy in copies:
            copy.wait()

    out = pl.pallas_call(
        body,
        out_shape=jax.ShapeDtypeStruct((PLANES - 1, 32, 8, SIDE), F32),
        in_specs=[pl.BlockSpec(memory_space=SMEM)] + [pl.BlockSpec(memory_space=pl.ANY)] * 2,
        out_specs=pl.BlockSpec(memory_space=pl.ANY),
        scratch_shapes=[pltpu.SemaphoreType.DMA((12,))],
        compiler_params=pltpu.CompilerParams(vmem_limit_bytes=SMALL),
        name="join_halves",
    )(place, mine, other)
    return out.reshape(MODES, 2, SIDE, SIDE)


def after(value, *events):
    def body(*refs):
        pass

    return pl.pallas_call(
        body,
        out_shape=jax.ShapeDtypeStruct(value.shape, value.dtype),
        in_specs=[pl.BlockSpec(memory_space=pl.ANY)] * (1 + len(events)),
        out_specs=pl.BlockSpec(memory_space=pl.ANY),
        input_output_aliases={0: 0},
        compiler_params=pltpu.CompilerParams(vmem_limit_bytes=SMALL),
        name="after",
    )(value, *events)


def add_corner(lower, left, *before):
    def body(lower_ref, left_ref, *refs):
        refs[-1][...] = lower_ref[...] + left_ref[:, SIDE:, :]

    return small_call(
        body, "add_corner", jax.ShapeDtypeStruct(lower.shape, F32), (lower, left, *before), unread=len(before)
    )


def update_object(own, core, left, above, weight):
    def body(own_ref, core_ref, left_ref, above_ref, weight_ref, out):
        scale = 1.0 / weight_ref[...]
        for part in range(2):
            block = own_ref[part] + core_ref[part]
            out[part] = (block + left_ref[part, :SIDE, :] + above_ref[part]) * scale

    return small_call(
        body, "update_object", jax.ShapeDtypeStruct(own.shape, F32), (own, core, left, above, weight)
    )


def shards(object_field, probe, amplitudes, positions, counts):
    row_id = lax.axis_index("gy")
    col_id = lax.axis_index("gx")
    core = row_id % 2
    x_at = row_id // 4
    y_at = (row_id // 2) % 2 * 2 + col_id // 8
    place = jnp.stack([row_id, col_id, core, x_at, y_at]).astype(jnp.int32)
    table = jnp.asarray(transform_tables())
    order = jnp.asarray(order_table())

    points = positions[0, 0]
    right_strip = [shifted(object_field[part : part + 1], "gx", -1) for part in range(2)]
    lower_strip = shifted(object_field, "gy", -1)
    points_left = shifted(points, "gx", 1)
    amplitude = sort_amplitude(amplitudes[0, 0], order)
    points_pair = shifted(jnp.concatenate([points, points_left], 0), "gy", 1)
    right_strip[0] = after(right_strip[0], amplitude, points_pair, place)
    diagonal = [shifted(strip, "gy", -1) for strip in right_strip]
    weight, old_rows = cover(place, counts, points, points_left, points_pair, probe)
    core_grad, side_grad, lower_grad, other_half, half = visit_patterns(
        place, counts, points, object_field, right_strip, lower_strip, diagonal, probe, amplitude, table,
        weight, old_rows,
    )

    half_in = send(other_half, core_pair())
    from_left = shifted(side_grad, "gx", 1)
    parts = scatter_sum(3, place, [half, half_in])
    arrived = [send(parts[step], x_ring(step)) for step in (1, 2, 3)]
    parts = scatter_sum(4, place, [parts[0]] + arrived)
    arrived = [send(parts[step], y_ring(step)) for step in (1, 2, 3)]
    block = plain_sum([parts[0]] + arrived)
    from_above = shifted(add_corner(lower_grad, from_left, block), "gy", 1)
    block = plain_sum([block, send(block, depth_pair())])
    fours = [send(block, depth_ring(step)) for step in (2, 4, 6)]
    chunk = swap_in_plane(update_probe([block] + fours, old_rows, from_above))
    new_object = update_object(object_field, core_grad, from_left, from_above, weight)
    new_probe = join_halves(place, chunk, send(chunk, core_pair()))
    return (new_object, new_probe)


def solution(mesh):
    in_specs = (
        P(None, "gy", "gx"),
        P(),
        P("gy", "gx", None, None, None),
        P("gy", "gx", None, None),
        P(),
    )
    out_specs = (P(None, "gy", "gx"), P())
    return jax.shard_map(shards, mesh=mesh, in_specs=in_specs, out_specs=out_specs, check_vma=False)
```

```python
import math

import jax
import jax.numpy as jnp
import numpy as np
from jax import lax
from jax.experimental import pallas as pl
from jax.experimental.pallas import tpu as pltpu
from jax.sharding import PartitionSpec as P

SIDE = 256
HALF = 128
MODES = 3
SLOTS = 4
PLANES = 2 * MODES + 1
AXES = ("gx", "gy")
SMALL = 16 * 1024 * 1024
LARGE = 40 * 1024 * 1024
VMEM = pltpu.VMEM
SMEM = pltpu.SMEM
F32 = jnp.float32
BF16 = jnp.bfloat16


def flat_index(x, y, z, core):
    return ((y % 2) * 8 + z) * 16 + x * 4 + (y // 2) * 2 + core


def routes(move):
    pairs = []
    for x in range(4):
        for y in range(4):
            for z in range(8):
                for core in range(2):
                    tx, ty, tz, tc = move(x, y, z, core)
                    pairs.append((flat_index(x, y, z, core), flat_index(tx % 4, ty % 4, tz % 8, tc % 2)))
    return pairs


def x_ring(step):
    return routes(lambda x, y, z, c: (x + step, y, z, c))


def y_ring(step):
    return routes(lambda x, y, z, c: (x, y + step, z, c))


def depth_ring(step):
    return routes(lambda x, y, z, c: (x, y, z + step, c))


def depth_pair():
    return routes(lambda x, y, z, c: (x, y, z ^ 1, c))


def core_pair():
    return routes(lambda x, y, z, c: (x, y, z, 1 - c))


def plane_groups():
    return [
        [flat_index(x, y, z, core) for x in range(4) for y in range(4)] for z in range(8) for core in range(2)
    ]


def swap_in_plane(value):
    return lax.all_to_all(value, AXES, split_axis=0, concat_axis=0, tiled=True, axis_index_groups=plane_groups())


def send(value, pairs):
    return lax.ppermute(value, AXES, pairs)


def shifted(value, axis, steps):
    count = lax.axis_size(axis)
    return lax.ppermute(value, axis, [(source, (source + steps) % count) for source in range(count)])


def split_table(matrix):
    high = matrix.astype(np.float32).astype(jnp.bfloat16)
    low = (matrix - high.astype(np.float64)).astype(jnp.bfloat16)
    return high, low


def transform_tables():
    n = np.arange(HALF)[:, None].astype(np.int64)
    k = np.arange(HALF)[None, :].astype(np.int64)
    tables = []
    for odd in (0, 1):
        angle = (n * (2 * k + odd) % SIDE) * (-2.0 * math.pi / SIDE)
        cos, sin = np.cos(angle) / 16.0, np.sin(angle) / 16.0
        right = np.block([[cos, sin], [-sin, cos]])
        for matrix in (right, right.T):
            tables.extend(split_table(matrix))
    return np.stack(tables)


def order_table():
    table = np.zeros((SIDE, SIDE), np.float32)
    order = np.concatenate([np.arange(0, SIDE, 2), np.arange(1, SIDE, 2)])
    table[order, np.arange(SIDE)] = 1.0
    return table.astype(jnp.bfloat16)


def split(value):
    high = value.astype(BF16)
    low = (value - high.astype(F32)).astype(BF16)
    return high, low


def dot(left, right):
    return jnp.dot(left, right, preferred_element_type=F32)


STEP = 64
LAG = 6


def add_split(parts, even, odd):
    for index, value in enumerate((even, odd)):
        high, low = split(value)
        parts[2 * index].append(high)
        parts[2 * index + 1].append(low)


def run_staggered(chains):
    step = 0
    while chains:
        for index, chain in enumerate(list(chains)):
            if chain is not None and step >= index * LAG:
                if next(chain, "end") == "end":
                    chains[index] = None
        step += 1
        if all(chain is None for chain in chains):
            return


def lanes(*parts):
    return jnp.concatenate(parts, axis=1)


def rows(*parts):
    return jnp.concatenate(parts, axis=0)


def cut_parts(value):
    def body(value_ref, real, imag, sems):
        copies = [
            pltpu.make_async_copy(value_ref.at[pl.ds(part, 1)], out, sems.at[part])
            for part, out in enumerate((real, imag))
        ]
        for copy in copies:
            copy.start()
        for copy in copies:
            copy.wait()

    part = jax.ShapeDtypeStruct((1,) + value.shape[1:], value.dtype)
    return pl.pallas_call(
        body,
        out_shape=(part, part),
        in_specs=[pl.BlockSpec(memory_space=pl.ANY)],
        out_specs=(pl.BlockSpec(memory_space=pl.ANY),) * 2,
        scratch_shapes=[pltpu.SemaphoreType.DMA((2,))],
        compiler_params=pltpu.CompilerParams(vmem_limit_bytes=SMALL),
        name="cut_parts",
    )(value)


def sort_kernel(amplitude, order, amp_out, measured, sems):
    loads = [
        pltpu.make_async_copy(
            amplitude.at[:, :, pl.ds(block * HALF, HALF)], measured.at[:, block], sems.at[block]
        )
        for block in range(2)
    ]
    for load in loads:
        load.start()
    for load in loads:
        load.wait()
    for item in range(SLOTS):
        sorted_rows = lanes(
            *[
                rows(*[measured[item, block, pl.ds(odd, HALF, stride=2), :] for odd in range(2)])
                for block in range(2)
            ]
        )
        high, rest = split(sorted_rows)
        rest32 = sorted_rows - high.astype(F32)
        middle, low = split(rest32)
        amp_out[item] = dot(high, order[...]) + (dot(middle, order[...]) + dot(low, order[...]))


def sort_amplitude(amplitude, order):
    return pl.pallas_call(
        sort_kernel,
        out_shape=jax.ShapeDtypeStruct((SLOTS, SIDE, SIDE), F32),
        in_specs=[pl.BlockSpec(memory_space=pl.ANY), pl.BlockSpec(memory_space=VMEM)],
        out_specs=pl.BlockSpec(memory_space=VMEM),
        scratch_shapes=[VMEM((SLOTS, 2, SIDE, HALF), F32), pltpu.SemaphoreType.DMA((2,))],
        compiler_params=pltpu.CompilerParams(vmem_limit_bytes=SMALL),
        cost_estimate=pl.CostEstimate(flops=2_000_000_000, bytes_accessed=4_000_000, transcendentals=0),
        name="sort_amplitude",
    )(amplitude, order)


def cover_kernel(place, counts, own, left, above, probe, weight_out, rows_out, doubled):
    start = pl.multiple_of((place[2] * 16 + place[3] * 4 + place[4]) * 8, 8)
    for mode in range(MODES):
        for part in range(2):
            rows_out[0, 2 * mode + part] = probe[mode, part, pl.ds(start, 8), :]
    coverage = probe[0, 0] * probe[0, 0]
    for mode in range(MODES):
        for part in range(2):
            if mode or part:
                coverage = coverage + probe[mode, part] * probe[mode, part]
    for block in range(2):
        for start in (0, SIDE):
            doubled[block, pl.ds(start, SIDE), :] = coverage[:, block * HALF : (block + 1) * HALF]
    row_id = place[0]
    col_id = place[1]
    row_iota = lax.broadcasted_iota(jnp.int32, (SIDE, SIDE), 0)
    lane_iota = lax.broadcasted_iota(jnp.int32, (SIDE, SIDE), 1)
    weight_out[...] = jnp.ones((SIDE, SIDE), F32)
    for up, back, points, skip in ((0, 0, own, 0), (0, 1, left, 0), (1, 0, above, 0), (1, 1, above, SLOTS)):
        tile_row = row_id - up
        tile_col = col_id - back
        inside = jnp.logical_and(tile_row >= 0, tile_col >= 0)
        count = jnp.where(inside, counts[jnp.maximum(tile_row, 0), jnp.maximum(tile_col, 0)], 0)

        def visit(item, carry, points=points, skip=skip, tile_row=tile_row, tile_col=tile_col, up=up, back=back):
            row_at = points[skip + item, 0] - tile_row * SIDE
            col_at = points[skip + item, 1] - tile_col * SIDE
            window = pl.ds(SIDE - row_at, SIDE)
            moved = pltpu.roll(lanes(doubled[0, window, :], doubled[1, window, :]), col_at, 1)
            row_ok = row_iota < row_at if up else row_iota >= row_at
            col_ok = lane_iota < col_at if back else lane_iota >= col_at
            weight_out[...] += jnp.where(jnp.logical_and(row_ok, col_ok), moved, 0.0)
            return carry

        lax.fori_loop(0, count, visit, 0)


def cover(place, counts, own, left, above, probe):
    return pl.pallas_call(
        cover_kernel,
        out_shape=(
            jax.ShapeDtypeStruct((SIDE, SIDE), F32),
            jax.ShapeDtypeStruct((1, PLANES - 1, 8, SIDE), F32),
        ),
        in_specs=[pl.BlockSpec(memory_space=SMEM)] * 5 + [pl.BlockSpec(memory_space=VMEM)],
        out_specs=(pl.BlockSpec(memory_space=VMEM),) * 2,
        scratch_shapes=[VMEM((2, 2 * SIDE, HALF), F32)],
        compiler_params=pltpu.CompilerParams(vmem_limit_bytes=SMALL),
        cost_estimate=pl.CostEstimate(flops=2_000_000_000, bytes_accessed=4_000_000, transcendentals=0),
        name="cover",
    )(place, counts, own, left, above, probe)


def pattern_kernel(
    place, counts, points, own, right_real, right_imag, lower, corner_real, corner_imag, probe, amplitude, table, weight, old_rows,
    core_out, right_out, lower_out, send_out, keep_out,
    field, target, total, spectrum, sems,
):
    row_id = place[0]
    col_id = place[1]
    core = place[2]
    loads = []
    for piece, part, length, up, back in (
        (own, 0, 2, 0, 0), (lower, 0, 2, 1, 0),
        (right_real, 0, 1, 0, 1), (right_imag, 1, 1, 0, 1),
        (corner_real, 0, 1, 1, 1), (corner_imag, 1, 1, 1, 1),
    ):
        for block in range(2):
            loads.append(
                pltpu.make_async_copy(
                    piece.at[:, :, pl.ds(block * HALF, HALF)],
                    field.at[pl.ds(part, length), 2 * back + block, pl.ds(up * SIDE, SIDE), :],
                    sems.at[len(loads)],
                )
            )
    for load in loads:
        load.start()
    target[...] = jnp.zeros_like(target)
    total[...] = jnp.zeros_like(total)
    for load in loads:
        load.wait()
    lane_iota = lax.broadcasted_iota(jnp.int32, (SIDE, SIDE), 1)

    def visit(item, carry):
        row_at = points[item, 0] - row_id * SIDE
        col_at = points[item, 1] - col_id * SIDE
        in_left = lane_iota >= col_at
        rest = jnp.where(col_at == 0, 0, SIDE - col_at)

        def cut(part):
            window = pl.ds(row_at, SIDE)
            first = lanes(field[part, 0, window, :], field[part, 1, window, :])
            second = lanes(field[part, 2, window, :], field[part, 3, window, :])
            return pltpu.roll(jnp.where(in_left, first, second), rest, 1)

        object_real = cut(0)
        object_imag = cut(1)
        density = object_real * object_real + object_imag * object_imag
        total[:, PLANES - 1] += density.reshape(32, 8, SIDE)

        sums = {}

        def forward(mode):
            probe_real = probe[mode, 0]
            probe_imag = probe[mode, 1]
            parts = [[], [], [], []]
            for at in range(0, SIDE, STEP):
                cut_rows = slice(at, at + STEP)
                p_real, p_imag = probe_real[cut_rows], probe_imag[cut_rows]
                o_real, o_imag = object_real[cut_rows], object_imag[cut_rows]
                real = p_real * o_real - p_imag * o_imag
                imag = p_real * o_imag + p_imag * o_real
                both = lanes(real[:, :HALF], imag[:, :HALF]), lanes(real[:, HALF:], imag[:, HALF:])
                add_split(parts, both[0] + both[1], both[0] - both[1])
                yield
            high, low, odd_high, odd_low = [rows(*part) for part in parts]
            even = dot(lanes(low, high, high), rows(table[0], table[1], table[0]))
            yield
            odd = dot(lanes(odd_low, odd_high, odd_high), rows(table[4], table[5], table[4]))
            yield
            parts = [[], [], [], []]
            for lane in (slice(0, HALF), slice(HALF, SIDE)):
                for at in range(0, HALF, STEP // 2):
                    top, bottom = slice(at, at + STEP // 2), slice(HALF + at, HALF + at + STEP // 2)
                    first = lanes(even[top, lane], odd[top, lane])
                    second = lanes(even[bottom, lane], odd[bottom, lane])
                    add_split(parts, first + second, first - second)
                    yield
            high, low, odd_high, odd_low = [rows(*part) for part in parts]
            even = dot(lanes(table[2], table[3], table[2]), rows(low, high, high))
            yield
            odd = dot(lanes(table[6], table[7], table[6]), rows(odd_low, odd_high, odd_high))
            yield
            for index, values in enumerate((even, odd)):
                spectrum[mode, index] = values
                power = values[:HALF] * values[:HALF] + values[HALF:] * values[HALF:]
                sums[index] = sums[index] + power if index in sums else power
                yield

        run_staggered([forward(mode) for mode in range(MODES)])
        factors = []
        for index in range(2):
            factor = amplitude[item, index * HALF : index * HALF + HALF] * lax.rsqrt(jnp.maximum(sums[index], 0.25))
            factors.append(rows(factor, factor))
        grads = []

        def backward(mode):
            halves = []
            for index in range(2):
                parts = [[], []]
                for at in range(0, SIDE, STEP):
                    cut_rows = slice(at, at + STEP)
                    value = spectrum[mode, index, pl.ds(at, STEP), :] * factors[index][cut_rows]
                    high, low = split(value)
                    parts[0].append(high)
                    parts[1].append(low)
                    yield
                halves.append([rows(*part) for part in parts])
            (high, low), (odd_high, odd_low) = halves
            even = dot(lanes(table[0], table[1], table[0]), rows(low, high, high))
            yield
            odd = dot(lanes(table[4], table[5], table[4]), rows(odd_low, odd_high, odd_high))
            yield
            parts = [[], [], [], []]
            for sign in (1, -1):
                for at in range(0, HALF, STEP // 2):
                    real, imag = slice(at, at + STEP // 2), slice(HALF + at, HALF + at + STEP // 2)
                    if sign == 1:
                        first, second = even[real] + odd[real], even[imag] + odd[imag]
                    else:
                        first, second = even[real] - odd[real], even[imag] - odd[imag]
                    add_split(
                        parts, lanes(first[:, :HALF], second[:, :HALF]), lanes(first[:, HALF:], second[:, HALF:])
                    )
                    yield
            high, low, odd_high, odd_low = [rows(*part) for part in parts]
            even = dot(lanes(low, high, high), rows(table[2], table[3], table[2]))
            yield
            odd = dot(lanes(odd_low, odd_high, odd_high), rows(table[6], table[7], table[6]))
            yield
            pieces = []
            for at in range(0, SIDE, STEP):
                cut_rows = slice(at, at + STEP)
                first, second = even[cut_rows] + odd[cut_rows], even[cut_rows] - odd[cut_rows]
                real = lanes(first[:, :HALF], second[:, :HALF])
                imag = lanes(first[:, HALF:], second[:, HALF:])
                p_real, p_imag = probe[mode, 0, pl.ds(at, STEP), :], probe[mode, 1, pl.ds(at, STEP), :]
                o_real, o_imag = object_real[cut_rows], object_imag[cut_rows]
                pieces.append((p_real * real + p_imag * imag, p_real * imag - p_imag * real))
                groups = pl.ds(at // 8, STEP // 8)
                total[groups, 2 * mode] += (o_real * real + o_imag * imag).reshape(STEP // 8, 8, SIDE)
                total[groups, 2 * mode + 1] += (o_real * imag - o_imag * real).reshape(STEP // 8, 8, SIDE)
                yield
            grads.append([rows(*[piece[part] for piece in pieces]) for part in range(2)])

        run_staggered([backward(mode) for mode in range(MODES)])
        grad_real = grads[0][0] + grads[1][0] + grads[2][0]
        grad_imag = grads[0][1] + grads[1][1] + grads[2][1]
        for part, grad in ((0, grad_real), (1, grad_imag)):
            moved = pltpu.roll(grad, col_at, 1)
            first = jnp.where(in_left, moved, 0.0)
            second = jnp.where(in_left, 0.0, moved)
            window = pl.ds(row_at, SIDE)
            for block, piece in enumerate((first[:, :HALF], first[:, HALF:], second[:, :HALF], second[:, HALF:])):
                target[part, block, window, :] += piece
        return carry

    lax.fori_loop(0, counts[row_id, col_id], visit, 0)
    stores = [
        pltpu.make_async_copy(total.at[pl.ds((1 - core) * 16, 16)], send_out, sems.at[0]),
        pltpu.make_async_copy(total.at[pl.ds(core * 16, 16)], keep_out, sems.at[1]),
    ]
    for piece, up, tall, back in ((core_out, 0, 1, 0), (right_out, 0, 2, 1), (lower_out, 1, 1, 0)):
        for block in range(2):
            stores.append(
                pltpu.make_async_copy(
                    target.at[:, 2 * back + block, pl.ds(up * SIDE, tall * SIDE), :],
                    piece.at[:, :, pl.ds(block * HALF, HALF)],
                    sems.at[len(stores)],
                )
            )
    for store in stores:
        store.start()
    for store in stores:
        store.wait()


def visit_patterns(place, counts, points, own, right, lower, corner, probe, amplitude, table, *before):
    tile = jax.ShapeDtypeStruct((2, SIDE, SIDE), F32)
    tall = jax.ShapeDtypeStruct((2, 2 * SIDE, SIDE), F32)
    part = jax.ShapeDtypeStruct((16, PLANES, 8, SIDE), F32)
    return pl.pallas_call(
        pattern_kernel,
        out_shape=(tile, tall, tile, part, part),
        in_specs=[pl.BlockSpec(memory_space=SMEM)] * 3
        + [pl.BlockSpec(memory_space=pl.ANY)] * 6
        + [pl.BlockSpec(memory_space=VMEM)] * 3
        + [pl.BlockSpec(memory_space=pl.ANY)] * 2,
        out_specs=(pl.BlockSpec(memory_space=pl.ANY),) * 5,
        scratch_shapes=[
            VMEM((2, 4, 2 * SIDE, HALF), F32),
            VMEM((2, 4, 2 * SIDE, HALF), F32),
            VMEM((32, PLANES, 8, SIDE), F32),
            VMEM((MODES, 2, SIDE, SIDE), F32),
            pltpu.SemaphoreType.DMA((12,)),
        ],
        compiler_params=pltpu.CompilerParams(vmem_limit_bytes=LARGE),
        cost_estimate=pl.CostEstimate(flops=10_000_000_000, bytes_accessed=10_000_000, transcendentals=0),
        name="patterns",
    )(place, counts, points, own, *right, lower, *corner, probe, amplitude, table, *before)


def small_call(body, name, out_shape, operands, scalars=0, unread=0, **options):
    held = len(operands) - scalars - unread
    out_specs = jax.tree.map(lambda _: pl.BlockSpec(memory_space=VMEM), out_shape)
    return pl.pallas_call(
        body,
        out_shape=out_shape,
        in_specs=[pl.BlockSpec(memory_space=SMEM)] * scalars
        + [pl.BlockSpec(memory_space=VMEM)] * held
        + [pl.BlockSpec(memory_space=pl.ANY)] * unread,
        out_specs=out_specs,
        compiler_params=pltpu.CompilerParams(vmem_limit_bytes=SMALL),
        name=name,
        **options,
    )(*operands)


def plain_sum(pieces, *before):
    number = len(pieces)

    def body(*refs):
        block = refs[0][...]
        for piece in refs[1:number]:
            block = block + piece[...]
        refs[-1][...] = block

    return small_call(
        body, "plain_sum", jax.ShapeDtypeStruct(pieces[0].shape, F32), (*pieces, *before), unread=len(before)
    )


def scatter_sum(slot, place, pieces):
    length = pieces[0].shape[0] // 4
    shape = (length,) + pieces[0].shape[1:]
    number = len(pieces)

    def body(place, *refs):
        outs = refs[-4:]
        for step in range(4):
            start = lax.rem(place[slot] + step, 4) * length
            block = refs[0][pl.ds(start, length)]
            for piece in refs[1:number]:
                block = block + piece[pl.ds(start, length)]
            outs[step][...] = block

    return small_call(body, "scatter_sum", (jax.ShapeDtypeStruct(shape, F32),) * 4, (place, *pieces), scalars=1)


def update_probe(pieces, old, *before):
    number = len(pieces)

    def body(*refs):
        old_ref, out = refs[number], refs[-1]
        block = refs[0][0]
        for piece in refs[1:number]:
            block = block + piece[0]
        scale = 1.0 / (block[PLANES - 1] + 1.0)
        for plane in range(PLANES - 1):
            new = (old_ref[0, plane] + block[plane]) * scale
            for copy in range(16):
                out[copy, plane] = new

    return small_call(
        body, "update_probe", jax.ShapeDtypeStruct((16,) + old.shape[1:], F32), (*pieces, old, *before),
        unread=len(before),
    )


def join_halves(place, mine, other):
    def body(place, mine_ref, other_ref, out, sem):
        core = place[2]
        copies = []
        for piece, half in ((mine_ref, core), (other_ref, 1 - core)):
            for plane in range(PLANES - 1):
                copies.append(
                    pltpu.make_async_copy(
                        piece.at[:, plane], out.at[plane, pl.ds(half * 16, 16)], sem.at[len(copies)]
                    )
                )
        for copy in copies:
            copy.start()
        for copy in copies:
            copy.wait()

    out = pl.pallas_call(
        body,
        out_shape=jax.ShapeDtypeStruct((PLANES - 1, 32, 8, SIDE), F32),
        in_specs=[pl.BlockSpec(memory_space=SMEM)] + [pl.BlockSpec(memory_space=pl.ANY)] * 2,
        out_specs=pl.BlockSpec(memory_space=pl.ANY),
        scratch_shapes=[pltpu.SemaphoreType.DMA((12,))],
        compiler_params=pltpu.CompilerParams(vmem_limit_bytes=SMALL),
        name="join_halves",
    )(place, mine, other)
    return out.reshape(MODES, 2, SIDE, SIDE)


def after(value, *events):
    def body(*refs):
        pass

    return pl.pallas_call(
        body,
        out_shape=jax.ShapeDtypeStruct(value.shape, value.dtype),
        in_specs=[pl.BlockSpec(memory_space=pl.ANY)] * (1 + len(events)),
        out_specs=pl.BlockSpec(memory_space=pl.ANY),
        input_output_aliases={0: 0},
        compiler_params=pltpu.CompilerParams(vmem_limit_bytes=SMALL),
        name="after",
    )(value, *events)


def add_corner(lower, left, *before):
    def body(lower_ref, left_ref, *refs):
        refs[-1][...] = lower_ref[...] + left_ref[:, SIDE:, :]

    return small_call(
        body, "add_corner", jax.ShapeDtypeStruct(lower.shape, F32), (lower, left, *before), unread=len(before)
    )


def update_object(own, core, left, above, weight):
    def body(own_ref, core_ref, left_ref, above_ref, weight_ref, out):
        scale = 1.0 / weight_ref[...]
        for part in range(2):
            block = own_ref[part] + core_ref[part]
            out[part] = (block + left_ref[part, :SIDE, :] + above_ref[part]) * scale

    return small_call(
        body, "update_object", jax.ShapeDtypeStruct(own.shape, F32), (own, core, left, above, weight)
    )


def shards(object_field, probe, amplitudes, positions, counts):
    row_id = lax.axis_index("gy")
    col_id = lax.axis_index("gx")
    core = row_id % 2
    x_at = row_id // 4
    y_at = (row_id // 2) % 2 * 2 + col_id // 8
    place = jnp.stack([row_id, col_id, core, x_at, y_at]).astype(jnp.int32)
    table = jnp.asarray(transform_tables())
    order = jnp.asarray(order_table())

    points = positions[0, 0]
    right_strip = [shifted(part, "gx", -1) for part in cut_parts(object_field)]
    lower_strip = shifted(object_field, "gy", -1)
    points_left = shifted(points, "gx", 1)
    amplitude = sort_amplitude(amplitudes[0, 0], order)
    points_pair = shifted(jnp.concatenate([points, points_left], 0), "gy", 1)
    right_strip[0] = after(right_strip[0], amplitude, points_pair, place)
    diagonal = [shifted(strip, "gy", -1) for strip in right_strip]
    weight, old_rows = cover(place, counts, points, points_left, points_pair, probe)
    core_grad, side_grad, lower_grad, other_half, half = visit_patterns(
        place, counts, points, object_field, right_strip, lower_strip, diagonal, probe, amplitude, table,
        weight, old_rows,
    )

    half_in = send(other_half, core_pair())
    from_left = shifted(side_grad, "gx", 1)
    parts = scatter_sum(3, place, [half, half_in])
    arrived = [send(parts[step], x_ring(step)) for step in (1, 2, 3)]
    parts = scatter_sum(4, place, [parts[0]] + arrived)
    arrived = [send(parts[step], y_ring(step)) for step in (1, 2, 3)]
    block = plain_sum([parts[0]] + arrived)
    from_above = shifted(add_corner(lower_grad, from_left, block), "gy", 1)
    block = plain_sum([block, send(block, depth_pair())])
    fours = [send(block, depth_ring(step)) for step in (2, 4, 6)]
    chunk = swap_in_plane(update_probe([block] + fours, old_rows, from_above))
    new_object = update_object(object_field, core_grad, from_left, from_above, weight)
    new_probe = join_halves(place, chunk, send(chunk, core_pair()))
    return (new_object, new_probe)


def solution(mesh):
    in_specs = (
        P(None, "gy", "gx"),
        P(),
        P("gy", "gx", None, None, None),
        P("gy", "gx", None, None),
        P(),
    )
    out_specs = (P(None, "gy", "gx"), P())
    return jax.shard_map(shards, mesh=mesh, in_specs=in_specs, out_specs=out_specs, check_vma=False)
```
